256 devices in a mesh: seq: 32 (over z, x), vocab: 8 (over y, core).
Axes of the slice: x: 4, y: 4, z: 8, core: 2. Of those that a mesh axis runs over, the one named last changes fastest.
Arguments:
- hidden: bfloat16 [512, 5120], P(('seq', 'vocab')), may hold values from -400 to 400
- norm_gain: float32 [5120], replicated, may hold values from 0.1 to 1.9
- head_weight: bfloat16 [5120, 131072], P(None, ('seq', 'vocab')), may hold values from -2 to 2
- teacher_logits: bfloat16 [1024, 32, 4096], P('seq', None, 'vocab'), may hold values from -12 to 300
- teacher_slot: int32 [512], replicated, may hold values from 0 to 1023, as said below
- valid_tokens: int32 [512], replicated, may hold values 0 or 1
Outputs:
- grad_hidden: bfloat16 [512, 5120], P(('seq', 'vocab'))
- grad_head: bfloat16 [5120, 131072], P(None, ('seq', 'vocab'))
The draws below stay inside these ranges and needn't reach their ends.
Inputs may be any that keep to these rules, and one draw needn't show every extreme that they name: `teacher_slot`: rows use distinct slots; slots g * 32 to (g + 1) * 32 - 1 belong to sequence group g of the teacher's packing; at most 32 rows use one group's slots, and some group holds 32 in every draw.
All inputs are finite; a program needn't handle non-finite values.
Results may differ from the reference program's by a relative error of at most 0.02.
Values may be sent and summed in bfloat16 or wider, within the bound.
A program may use at most 128 MiB of HBM per device.

```python
import math
import jax
import jax.numpy as jnp
from jax import lax

D = 5120
ROWS = 512
VSPAN = 4096
VOCAB = 131072
TCAP = 32
N_SEQ = 32


def slot_map(key):
    key_group, key_order, key_within, key_others = jax.random.split(jax.random.fold_in(key, 31), 4)
    full_group = jax.random.randint(key_group, (), 0, N_SEQ)
    row_order = jax.random.permutation(key_order, ROWS)
    within = jax.random.permutation(key_within, TCAP)
    others = jax.random.permutation(key_others, (N_SEQ - 1) * TCAP)
    ranks = jnp.arange(ROWS, dtype=jnp.int32)
    full_part = full_group * TCAP + within[jnp.minimum(ranks, TCAP - 1)]
    other_index = others[jnp.clip(ranks - TCAP, 0, (N_SEQ - 1) * TCAP - 1)]
    other_part = (other_index // TCAP + full_group + 1) % N_SEQ * TCAP + other_index % TCAP
    by_rank = jnp.where(ranks < TCAP, full_part, other_part).astype(jnp.int32)
    return jnp.zeros((ROWS,), jnp.int32).at[row_order].set(by_rank)


def draw_teacher_slot(key, part):
    return slot_map(key)


def draw_hidden(key, part):
    key_base, key_row, key_column = jax.random.split(jax.random.fold_in(key, 11), 3)
    row_scale = jnp.exp(jax.random.uniform(key_row, (ROWS, 1), jnp.float32, 0.0, math.log(10.0)))
    column_scale = jnp.exp(jax.random.uniform(key_column, (1, D), jnp.float32, 0.0, math.log(10.0)))
    base_draw = jnp.clip(jax.random.normal(key_base, (ROWS, D), jnp.float32), -4.0, 4.0)
    values = base_draw * row_scale * column_scale
    return values.astype(jnp.bfloat16)


def draw_head_weight(key, part):
    key_main = jax.random.fold_in(key, 41)
    spread = 3.0 / math.sqrt(D)
    values = jnp.clip(jax.random.normal(key_main, (D, VOCAB), jnp.float32), -4.0, 4.0) * spread
    return values.astype(jnp.bfloat16)


def draw_teacher_logits(key, part):
    key_main = jax.random.fold_in(key, 23)
    draw_shape = (N_SEQ * TCAP, N_SEQ, VSPAN)
    values = jnp.clip(jax.random.normal(key_main, draw_shape, jnp.float32), -4.0, 4.0) * 3.0
    return values.astype(jnp.bfloat16)


def touch_ends(result, key, low, largest):
    place = [jax.random.randint(jax.random.fold_in(key, axis), (), 0, length) for axis, length in enumerate(result.shape)]
    longest = result.shape.index(max(result.shape))
    neighbour = place[:longest] + [(place[longest] + 1) % result.shape[longest]] + place[longest + 1:]
    return result.at[tuple(place)].set(low).at[tuple(neighbour)].set(largest)


def setup_inputs(seed: int = 0) -> dict:
    streams_of = jax.random.split(jax.random.key(seed), 7)
    hidden = draw_hidden(jax.random.fold_in(streams_of[6], 71), 0)
    norm_gain = jnp.clip(1.0 + 0.18 * jax.random.normal(streams_of[1], (D,), jnp.float32), 0.1, 1.9)
    head_weight = draw_head_weight(jax.random.fold_in(streams_of[6], 71), 0)
    teacher_logits = draw_teacher_logits(jax.random.fold_in(streams_of[6], 71), 0)
    teacher_slot = draw_teacher_slot(jax.random.fold_in(streams_of[6], 71), 0)
    valid_tokens = touch_ends((jax.random.randint(streams_of[5], (ROWS,), 0, 4) < 3).astype(jnp.int32), jax.random.fold_in(streams_of[5], 1), 0, 1)
    return dict(hidden=hidden, norm_gain=norm_gain, head_weight=head_weight, teacher_logits=teacher_logits, teacher_slot=teacher_slot, valid_tokens=valid_tokens)


epsilon = 1e-06

def block_grad(features, vocab_block):
    return jnp.dot(features.T, vocab_block, preferred_element_type=jnp.float32).astype(jnp.bfloat16)

def partial_grad(features):

    def apply_block(vocab_block):
        return block_grad(features, vocab_block)
    return apply_block

def reference(hidden, norm_gain, head_weight, teacher_logits, teacher_slot, valid_tokens):
    widened = hidden.astype(jnp.float32)
    inv_rms = lax.rsqrt(lax.optimization_barrier(jnp.mean(widened * widened, axis=1, keepdims=True)) + epsilon)
    normed = widened * inv_rms
    features = (normed * norm_gain).astype(jnp.bfloat16)
    logits = jnp.dot(features, head_weight, preferred_element_type=jnp.float32)
    slot_table = teacher_logits.reshape(N_SEQ * TCAP, VOCAB)
    teacher = jnp.take(slot_table, teacher_slot.astype(jnp.int32), axis=0).astype(jnp.float32)
    student_top = lax.optimization_barrier(jnp.max(logits, axis=1, keepdims=True))
    teacher_top = lax.optimization_barrier(jnp.max(teacher, axis=1, keepdims=True))
    shifted = jnp.exp(logits - student_top)
    student_total = lax.optimization_barrier(jnp.sum(shifted, axis=1, keepdims=True))
    teacher_total = lax.optimization_barrier(jnp.sum(jnp.exp(teacher - teacher_top), axis=1, keepdims=True))
    cross_sum = lax.optimization_barrier(jnp.sum(shifted * (logits - teacher), axis=1, keepdims=True))
    student_lse = student_top + jnp.log(student_total)
    teacher_lse = teacher_top + jnp.log(teacher_total)
    divergence = cross_sum / student_total - student_lse + teacher_lse
    student_prob = jnp.exp(logits - student_lse)
    log_gap = logits - student_lse - (teacher - teacher_lse)
    row_weight = valid_tokens.astype(jnp.float32)[:, None]
    logit_grad = (row_weight * student_prob * (log_gap - divergence)).astype(jnp.bfloat16)
    vocab_blocks = logit_grad.reshape(ROWS, N_SEQ, VSPAN).transpose(1, 0, 2)
    grad_blocks = lax.map(partial_grad(features), vocab_blocks)
    grad_head = grad_blocks.transpose(1, 0, 2).reshape(D, VOCAB)
    feature_grad = lax.dot_general(logit_grad, head_weight, (((1,), (1,)), ((), ())), preferred_element_type=jnp.float32)
    norm_grad = feature_grad * norm_gain
    grad_hidden = inv_rms * (norm_grad - normed * lax.optimization_barrier(jnp.mean(norm_grad * normed, axis=1, keepdims=True)))
    return (grad_hidden.astype(jnp.bfloat16), grad_head)
```

```python
import functools

import jax
import jax.numpy as jnp
from jax import lax
from jax.experimental import pallas as pl
from jax.experimental.pallas import tpu as pltpu
from jax.sharding import PartitionSpec as P

MESH = pl.DeviceIdType.MESH
F32 = jnp.float32
BF16 = jnp.bfloat16
epsilon = 1e-06

NZ, NX, NY, NC = 8, 4, 4, 2
NV, NS = NY * NC, NZ * NX
ROWS, D, CB, COLS = 512, 5120, 640, 512
NJ = 5
ORDER = (4, 0, 2, 1, 3)
XFIRST, YFIRST, ZFIRST = (0, 1), (2, 3), (4,)
N_SEM = 240


class Links:
    def __init__(self, send, recv):
        self.send, self.recv, self.used = send, recv, 0

    def take(self, count=1):
        first = self.used
        self.used += count
        assert self.used <= N_SEM
        return first

    def copy(self, src, dst, device, index=None):
        if index is None:
            index = self.take()
        return pltpu.make_async_remote_copy(
            src_ref=src,
            dst_ref=dst,
            send_sem=self.send.at[index],
            recv_sem=self.recv.at[index],
            device_id=device,
            device_id_type=MESH,
        )


def mod(value, n):
    return lax.rem(value, n)


def loop(count, body):
    def step(i, carry):
        body(i)
        return carry

    lax.fori_loop(0, count, step, 0)


def kernel(
    hid, gain, slot, valid, w_hbm, teach,
    gh_out, head_out,
    w, f, sf, rf, fa, t32, ts, tt, onehot, logits, trow, st, sa, sb, sc, grad,
    po, ps, cr, tx, rx, ty, ry, zr, ax, ay, az, t2, r2, tz2, rz2, a2, zz, a2z, yy, ra, sq, rq, stage,
    send, recv, wsem, osem,
):
    s = lax.axis_index("seq")
    v = lax.axis_index("vocab")
    z, x = lax.div(s, NX), mod(s, NX)
    y, c = lax.div(v, NC), mod(v, NC)
    links = Links(send, recv)

    def at_s(other):
        return (other, v)

    def at_v(other):
        return (s, other)

    def at_z(other):
        return (other * NX + x, v)

    def at_x(other):
        return (z * NX + other, v)

    def at_y(other):
        return (s, other * NC + c)

    wcopy = pltpu.make_async_copy(w_hbm, w, wsem)
    wcopy.start()

    barrier = pltpu.get_barrier_semaphore()

    def greet_seq(k):
        pl.semaphore_signal(barrier, inc=1, device_id=at_s(mod(s + k + 1, NS)), device_id_type=MESH)

    def greet_vocab(k):
        pl.semaphore_signal(barrier, inc=1, device_id=at_v(mod(v + k + 1, NV)), device_id_type=MESH)

    loop(NV - 1, greet_vocab)
    loop(NS - 1, greet_seq)

    h = hid[...].astype(F32)
    inv_rms = lax.rsqrt(jnp.mean(h * h, axis=1, keepdims=True) + epsilon)
    for b in range(NV):
        part = h[:, b * CB:(b + 1) * CB] * inv_rms * gain[b]
        sf[b] = part.astype(BF16).astype(F32)
    rf[v] = sf[v]
    pl.semaphore_wait(barrier, NV - 1 + NS - 1)

    first = links.take(NV)

    def block_copy(k):
        to = mod(v + k, NV)
        return links.copy(sf.at[to], rf.at[v], at_v(to), first + k)

    def block_arrival(k):
        source = mod(v + NV - k, NV)
        return links.copy(sf.at[source], rf.at[source], at_v(source), first + k)

    loop(NV - 1, lambda k: block_copy(k + 1).start())

    for b in range(4):
        t32[b] = teach[:, b * 128:(b + 1) * 128].astype(F32)
    teach_first = links.take(NS)

    def arrange(d):
        for b in range(4):
            ts[d, :, b * 128:(b + 1) * 128] = t32[b, pl.ds(d, 32, stride=NS), :].astype(BF16)

    loop(NS, arrange)

    loop(NV - 1, lambda k: block_arrival(k + 1).wait_recv())
    for b in range(NV):
        fa[2 * b:2 * b + 2, :] = rf[b]
    f[v, z, x] = fa[...].astype(BF16)

    z_first = links.take(NZ)

    def z_copy(k):
        return links.copy(f.at[v, z, x], f.at[v, z, x], at_z(mod(z + k, NZ)), z_first + k)

    def z_arrival(k):
        source = mod(z + NZ - k, NZ)
        return links.copy(f.at[v, source, x], f.at[v, source, x], at_z(source), z_first + k)

    loop(NZ - 1, lambda k: z_copy(k + 1).start())

    def teach_copy(k):
        to = mod(s + k, NS)
        return links.copy(ts.at[to], tt.at[s], at_s(to), teach_first + k)

    def teach_arrival(k):
        source = mod(s + NS - k, NS)
        return links.copy(ts.at[source], tt.at[source], at_s(source), teach_first + k)

    loop(NS - 1, lambda k: teach_copy(k + 1).start())
    tt[s] = ts[s]

    slot_column = jnp.broadcast_to(slot[...].astype(F32), (128, ROWS)).T
    lane = lax.broadcasted_iota(jnp.int32, (ROWS, 128), 1).astype(F32)
    for b in range(8):
        onehot[:, b * 128:(b + 1) * 128] = jnp.where(slot_column == lane + float(b * 128), 1.0, 0.0).astype(BF16)

    loop(NZ - 1, lambda k: z_arrival(k + 1).wait_recv())

    offsets = (0, 1, 3, 2)
    parts = [mod(x + NX - o, NX) for o in offsets]
    x_first = links.take(NX)

    def x_copy(o, part):
        return links.copy(f.at[v, :, part], f.at[v, :, part], at_x(mod(x + o, NX)), x_first + o)

    for o in (1, 3, 2):
        x_copy(o, x).start()
    up, down, far = mod(y + 1, NY), mod(y + 3, NY), mod(y + 2, NY)
    other_core = (s, y * NC + (1 - c))
    y_first = links.take(16)
    core_first = links.take(16)

    def y_copy(block_y, zs, part, to_y, index):
        ref = f.at[block_y * NC + c, zs[0]:zs[1], part]
        return links.copy(ref, ref, at_y(to_y), index)

    def core_send(rank, i, block_y):
        ref = f.at[block_y * NC + c, :, parts[i]]
        return links.copy(ref, ref, other_core, core_first + rank * 4 + i)

    def core_arrive(rank, i, block_y):
        ref = f.at[block_y * NC + 1 - c, :, parts[i]]
        return links.copy(ref, ref, other_core, core_first + rank * 4 + i)

    pending = []

    def go(copy):
        copy.start()
        pending.append(copy)

    for i, o in enumerate(offsets):
        if o:
            x_copy(o, parts[i]).wait_recv()
        go(y_copy(y, (0, NZ), parts[i], up, y_first + i))
        go(y_copy(y, (0, NZ), parts[i], down, y_first + 4 + i))
        go(core_send(0, i, y))
    for i in range(4):
        y_copy(down, (0, NZ), parts[i], up, y_first + i).wait_recv()
        go(y_copy(down, (0, 4), parts[i], up, y_first + 8 + i))
        go(core_send(1, i, down))
        y_copy(up, (0, NZ), parts[i], down, y_first + 4 + i).wait_recv()
        go(y_copy(up, (4, NZ), parts[i], down, y_first + 12 + i))
        go(core_send(2, i, up))

    wcopy.wait()

    def multiply(block_y, block_c, fresh=False):
        block = block_y * NC + block_c
        wb = w.at[block_y, block_c]

        def rows(i):
            fb = f[block, pl.ds(i * 4, 4)].reshape(256, CB)
            product = jnp.dot(fb, wb[...].reshape(CB, COLS), preferred_element_type=F32)
            span = pl.ds(pl.multiple_of(i * 256, 256), 256)
            if fresh:
                logits[span, :] = product
            else:
                logits[span, :] += product

        loop(2, rows)

    multiply(y, c, True)
    multiply(down, c)
    multiply(up, c)
    for i in range(4):
        y_copy(far, (0, 4), parts[i], up, y_first + 8 + i).wait_recv()
        y_copy(far, (4, NZ), parts[i], down, y_first + 12 + i).wait_recv()
        go(core_send(3, i, far))
    for rank, block_y in enumerate((y, down, up, far)):
        if rank == 3:
            multiply(far, c)
        for i in range(4):
            core_arrive(rank, i, block_y).wait_recv()
        multiply(block_y, 1 - c)

    loop(NS - 1, lambda k: teach_arrival(k + 1).wait_recv())

    def select(i):
        span = pl.ds(pl.multiple_of(i * 256, 256), 256)
        trow[span, :] = jnp.dot(onehot[span, :], tt[...].reshape(1024, COLS), preferred_element_type=F32)

    loop(2, select)

    def statistics(i):
        span = pl.ds(pl.multiple_of(i * 64, 64), 64)
        lo, te = logits[span, :], trow[span, :]
        top = jnp.max(lo, axis=1, keepdims=True)
        teacher_top = jnp.max(te, axis=1, keepdims=True)
        e = jnp.exp(lo - top)
        total = jnp.sum(e, axis=1, keepdims=True)
        cross = jnp.sum(e * (lo - te), axis=1, keepdims=True)
        teacher_total = jnp.sum(jnp.exp(te - teacher_top), axis=1, keepdims=True)
        column = lax.broadcasted_iota(jnp.int32, (64, 128), 1)
        packed = jnp.where(column == 0, top, jnp.where(column == 1, teacher_top, jnp.where(column == 2, total, jnp.where(
            column == 3, cross, jnp.where(column == 4, teacher_total, 0.0)))))
        st[span, :] = packed

    loop(8, statistics)

    def merged(ref):
        value = ref[...]
        top = jnp.max(value[:, 0:1, :], axis=0, keepdims=True)
        teacher_top = jnp.max(value[:, 1:2, :], axis=0, keepdims=True)
        scale = jnp.exp(value[:, 0:1, :] - top)
        teacher_scale = jnp.exp(value[:, 1:2, :] - teacher_top)
        total = jnp.sum(value[:, 2:3, :] * scale, axis=0)
        cross = jnp.sum(value[:, 3:4, :] * scale, axis=0)
        teacher_total = jnp.sum(value[:, 4:5, :] * teacher_scale, axis=0)
        return top[0], teacher_top[0], total, cross, teacher_total

    def exchange(buffer, here, count, device):
        start = links.take(count)

        def out(k):
            return links.copy(buffer.at[here], buffer.at[here], device(mod(here + k, count)), start + k)

        def arrival(k):
            source = mod(here + count - k, count)
            return links.copy(buffer.at[source], buffer.at[source], device(source), start + k)

        loop(count - 1, lambda k: out(k + 1).start())
        loop(count - 1, lambda k: arrival(k + 1).wait_recv())
        return lambda: loop(count - 1, lambda k: out(k + 1).wait_send())

    def put(buffer, here, rows):
        for r, row in enumerate(rows):
            buffer[here, r:r + 1, :] = row

    flushes = []
    sa[v] = st[...].T[0:8, :]
    flushes.append(exchange(sa, v, NV, at_v))
    put(sb, x, merged(sa))
    flushes.append(exchange(sb, x, NX, at_x))
    put(sc, z, merged(sb))
    flushes.append(exchange(sc, z, NZ, at_z))
    top, teacher_top, total, cross, teacher_total = merged(sc)
    student_lse = top + jnp.log(total)
    teacher_lse = teacher_top + jnp.log(teacher_total)
    divergence = cross / total - student_lse + teacher_lse
    quantity = lax.broadcasted_iota(jnp.int32, (128, ROWS), 0)
    st[...] = jnp.where(quantity == 0, student_lse, jnp.where(quantity == 1, teacher_lse, jnp.where(
        quantity == 2, divergence, valid[...].astype(F32)))).T

    def gradient(i):
        span = pl.ds(pl.multiple_of(i * 64, 64), 64)
        lo, te, q = logits[span, :], trow[span, :], st[span, :]
        shifted = lo - q[:, 0:1]
        gap = shifted - (te - q[:, 1:2])
        grad[span, :] = (q[:, 3:4] * jnp.exp(shifted) * (gap - q[:, 2:3])).astype(BF16)

    loop(8, gradient)

    def partial(j, half, ref):
        wj = w.at[:, half, j]

        def rows(i):
            g = grad[pl.ds(pl.multiple_of(i * 256, 256), 256), :]
            product = lax.dot_general(g, wj[...].reshape(4 * 128, COLS), (((1,), (1,)), ((), ())), preferred_element_type=F32)
            for b in range(NY):
                ref[j, b, pl.ds(i * 4, 4)] = product[:, b * 128:(b + 1) * 128].reshape(4, NX, 16, 128)

        loop(2, rows)

    def add_core(j):
        def step(i):
            ps[j, i] += cr[j, i]

        loop(NY, step)

    class Ring:
        def __init__(self, here, device, block, tmp, arrived):
            self.block, self.tmp, self.arrived, self.here = block, tmp, arrived, here
            up, down, far = mod(here + 1, 4), mod(here + 3, 4), mod(here + 2, 4)
            self.up, self.down = up, down
            self.far0 = links.copy(block(far, 0), tmp.at[0], device(up))
            self.far1 = links.copy(block(far, 1), tmp.at[1], device(down))
            self.free0 = links.copy(block(up, 1), arrived.at[0, 1], device(up))
            self.free1 = links.copy(block(down, 0), arrived.at[1, 0], device(down))
            self.last0 = links.copy(tmp.at[0], arrived.at[0, 0], device(up))
            self.last1 = links.copy(tmp.at[1], arrived.at[1, 1], device(down))
            for copy in (self.far0, self.far1, self.free0, self.free1):
                go(copy)

        def middle(self):
            self.far0.wait_recv()
            self.tmp[0] = self.tmp[0] + self.block(self.up, 0)[...]
            go(self.last0)
            self.far1.wait_recv()
            self.tmp[1] = self.tmp[1] + self.block(self.down, 1)[...]
            go(self.last1)

        def finish(self):
            for copy in (self.free0, self.free1, self.last0, self.last1):
                copy.wait_recv()
            return [self.block(self.here, i)[...] + self.arrived[0, i] + self.arrived[1, i] for i in (0, 1)]

    core_links = {j: links.copy(po.at[j], cr.at[j], other_core) for j in ORDER}
    stage1 = {}
    z_direct = links.take(NZ)

    def zr_copy(k):
        to = mod(z + k, NZ)
        return links.copy(ps.at[4, :, to], zr.at[z], at_z(to), z_direct + k)

    def zr_arrival(k):
        source = mod(z + NZ - k, NZ)
        return links.copy(ps.at[4, :, source], zr.at[source], at_z(source), z_direct + k)

    def begin(j):
        core_links[j].wait_recv()
        add_core(j)
        if j in XFIRST:
            stage1[j] = Ring(x, at_x, lambda i, half, j=j: ps.at[j, half * 2:half * 2 + 2, :, i], tx.at[j], rx.at[j])
        elif j in YFIRST:
            stage1[j] = Ring(y, at_y, lambda i, half, j=j: ps.at[j, i, half * 4:half * 4 + 4], ty.at[j - 2], ry.at[j - 2])
        else:
            loop(NZ - 1, lambda k: zr_copy(k + 1).start())

    for n, j in enumerate(ORDER):
        partial(j, 1 - c, po)
        go(core_links[j])
        partial(j, c, ps)
        if n:
            begin(ORDER[n - 1])
    begin(ORDER[-1])

    out_copies = [pltpu.make_async_copy(stage.at[b % 2], head_out.at[b], osem.at[b % 2]) for b in range(NV)]

    def head_block(b):
        if b >= 2:
            out_copies[b - 2].wait()

        fb = f[b].reshape(ROWS, CB)
        product = lax.dot_general(fb, grad[...], (((0,), (0,)), ((), ())), preferred_element_type=F32)
        stage[b % 2] = product.astype(BF16)
        out_copies[b].start()

    for b in range(4):
        head_block(b)
    for j in ORDER[1:]:
        stage1[j].middle()
    for b in range(4, NV):
        head_block(b)

    def spread(buffer, source, here, count, device):
        start = links.take(count)

        def out(k):
            to = mod(here + k, count)
            return links.copy(source.at[to], buffer.at[here], device(to), start + k)

        def arrival(k):
            other = mod(here + count - k, count)
            return links.copy(source.at[other], buffer.at[other], device(other), start + k)

        loop(count - 1, lambda k: out(k + 1).start())
        buffer[here] = source[here]
        flushes.append(lambda: loop(count - 1, lambda k: out(k + 1).wait_send()))
        return lambda: loop(count - 1, lambda k: arrival(k + 1).wait_recv())

    stage2, stage3 = {}, {}
    for j in ORDER[1:]:
        low, high = stage1[j].finish()
        if j in XFIRST:
            mine = ax.at[j]
            mine[0:2] = low
            mine[2:4] = high
            stage2[j] = Ring(y, at_y, lambda i, half, m=mine: m.at[i, half * 4:half * 4 + 4], t2.at[j], r2.at[j])
        else:
            mine = ay.at[j - 2]
            mine[0:4] = low
            mine[4:8] = high
            stage2[j] = Ring(x, at_x, lambda i, half, m=mine: m.at[half * 4:half * 4 + 4, i], t2.at[j], r2.at[j])
    loop(NZ - 1, lambda k: zr_arrival(k + 1).wait_recv())
    az[...] = ps[4, :, z]

    def add_z(k):
        az[...] += zr[mod(z + NZ - k - 1, NZ)]

    loop(NZ - 1, add_z)
    stage2[4] = Ring(x, at_x, lambda i, half: az.at[half * 2:half * 2 + 2, i], tz2, rz2)
    for j in (0, 2, 1, 3, 4):
        stage2[j].middle()
    for j in (0, 2, 1, 3, 4):
        low, high = stage2[j].finish()
        if j == 4:
            a2z[0:2] = low
            a2z[2:4] = high
            stage3[j] = spread(yy, a2z, y, NY, at_y)
        else:
            a2[j, 0:4] = low
            a2[j, 4:8] = high
            stage3[j] = spread(zz.at[j], a2.at[j], z, NZ, at_z)
    for j in (0, 2, 1, 3, 4):
        stage3[j]()
        arrived = yy[...] if j == 4 else zz[j]
        ra[:, j * 128:(j + 1) * 128] = jnp.sum(arrived, axis=0)
    for b in range(NV):
        sq[b] = ra[2 * b:2 * b + 2, :]
    spread(rq, sq, v, NV, at_v)()

    h = hid[...].astype(F32)
    inv_rms = lax.rsqrt(jnp.mean(h * h, axis=1, keepdims=True) + epsilon)
    dots = jnp.zeros((2, 1), F32)
    for b in range(NV):
        normed = h[:, b * CB:(b + 1) * CB] * inv_rms
        dots = dots + jnp.sum(rq[b] * gain[b] * normed, axis=1, keepdims=True)
    dots = dots / D
    for b in range(NV):
        normed = h[:, b * CB:(b + 1) * CB] * inv_rms
        gh_out[:, b * CB:(b + 1) * CB] = (inv_rms * (rq[b] * gain[b] - normed * dots)).astype(BF16)

    for copy in out_copies[NV - 2:]:
        copy.wait()
    for copy in pending:
        copy.wait_send()
    for o in (1, 3, 2):
        x_copy(o, x).wait_send()
    loop(NV - 1, lambda k: block_copy(k + 1).wait_send())
    loop(NZ - 1, lambda k: z_copy(k + 1).wait_send())
    loop(NZ - 1, lambda k: zr_copy(k + 1).wait_send())
    loop(NS - 1, lambda k: teach_copy(k + 1).wait_send())
    for flush in flushes:
        flush()


def shards(hidden, norm_gain, head_weight, teacher_logits, teacher_slot, valid_tokens):
    vmem = pl.BlockSpec(memory_space=pltpu.VMEM)
    hbm = pl.BlockSpec(memory_space=pl.ANY)
    scratch = [
        pltpu.VMEM((NY, NC, NJ, 128, COLS), BF16),
        pltpu.VMEM((NV, NZ, NX, 16, CB), BF16),
        pltpu.VMEM((NV, 2, CB), F32),
        pltpu.VMEM((NV, 2, CB), F32),
        pltpu.VMEM((16, CB), F32),
        pltpu.VMEM((4, 1024, 128), F32),
        pltpu.VMEM((NS, 32, COLS), BF16),
        pltpu.VMEM((NS, 32, COLS), BF16),
        pltpu.VMEM((ROWS, 1024), BF16),
        pltpu.VMEM((ROWS, COLS), F32),
        pltpu.VMEM((ROWS, COLS), F32),
        pltpu.VMEM((ROWS, 128), F32),
        pltpu.VMEM((NV, 8, ROWS), F32),
        pltpu.VMEM((NX, 8, ROWS), F32),
        pltpu.VMEM((NZ, 8, ROWS), F32),
        pltpu.VMEM((ROWS, COLS), BF16),
        pltpu.VMEM((NJ, NY, NZ, NX, 16, 128), F32),
        pltpu.VMEM((NJ, NY, NZ, NX, 16, 128), F32),
        pltpu.VMEM((NJ, NY, NZ, NX, 16, 128), F32),
        pltpu.VMEM((2, 2, 2, NZ, 16, 128), F32),
        pltpu.VMEM((2, 2, 2, 2, NZ, 16, 128), F32),
        pltpu.VMEM((2, 2, 4, NX, 16, 128), F32),
        pltpu.VMEM((2, 2, 2, 4, NX, 16, 128), F32),
        pltpu.VMEM((NZ, NY, NX, 16, 128), F32),
        pltpu.VMEM((2, NY, NZ, 16, 128), F32),
        pltpu.VMEM((2, NZ, NX, 16, 128), F32),
        pltpu.VMEM((NY, NX, 16, 128), F32),
        pltpu.VMEM((4, 2, 4, 16, 128), F32),
        pltpu.VMEM((4, 2, 2, 4, 16, 128), F32),
        pltpu.VMEM((2, 2, 16, 128), F32),
        pltpu.VMEM((2, 2, 2, 16, 128), F32),
        pltpu.VMEM((4, NZ, 16, 128), F32),
        pltpu.VMEM((4, NZ, 16, 128), F32),
        pltpu.VMEM((NY, 16, 128), F32),
        pltpu.VMEM((NY, 16, 128), F32),
        pltpu.VMEM((16, CB), F32),
        pltpu.VMEM((NV, 2, CB), F32),
        pltpu.VMEM((NV, 2, CB), F32),
        pltpu.VMEM((2, CB, COLS), BF16),
        pltpu.SemaphoreType.DMA((N_SEM,)),
        pltpu.SemaphoreType.DMA((N_SEM,)),
        pltpu.SemaphoreType.DMA,
        pltpu.SemaphoreType.DMA((2,)),
    ]
    grad_hidden, grad_head = pl.pallas_call(
        kernel,
        out_shape=(jax.ShapeDtypeStruct((2, D), BF16), jax.ShapeDtypeStruct((NV, CB, COLS), BF16)),
        in_specs=[vmem, vmem, vmem, vmem, hbm, vmem],
        out_specs=(vmem, hbm),
        scratch_shapes=scratch,
        compiler_params=pltpu.CompilerParams(
            collective_id=0, has_side_effects=True, vmem_limit_bytes=60 * 2**20
        ),
        name="distill_head",
    )(
        hidden,
        norm_gain.reshape(NV, 1, CB),
        teacher_slot.reshape(1, ROWS),
        valid_tokens.reshape(1, ROWS),
        head_weight.reshape(NY, NC, NJ, 128, COLS),
        teacher_logits.reshape(1024, COLS),
    )
    return grad_hidden, grad_head.reshape(D, COLS)


def solution(mesh):
    placed = (
        P(("seq", "vocab"), None),
        P(),
        P(None, ("seq", "vocab")),
        P("seq", None, "vocab"),
        P(),
        P(),
    )
    return jax.shard_map(
        shards,
        mesh=mesh,
        in_specs=placed,
        out_specs=(P(("seq", "vocab"), None), P(None, ("seq", "vocab"))),
        check_vma=False,
    )
```

```python
import functools

import jax
import jax.numpy as jnp
from jax import lax
from jax.experimental import pallas as pl
from jax.experimental.pallas import tpu as pltpu
from jax.sharding import PartitionSpec as P

MESH = pl.DeviceIdType.MESH
F32 = jnp.float32
BF16 = jnp.bfloat16
epsilon = 1e-06

NZ, NX, NY, NC = 8, 4, 4, 2
NV, NS = NY * NC, NZ * NX
ROWS, D, CB, SB, COLS = 512, 5120, 640, 1024, 512
HALF = ROWS // NC
NJ = 5
ORDER = (4, 0, 2, 1, 3)
XFIRST, YFIRST = (0, 1), (2, 3)
N_SEM = 240
EARLY = 4
SPLIT = 5


class Links:
    def __init__(self, send, recv):
        self.send, self.recv, self.used = send, recv, 0

    def take(self, count=1):
        first = self.used
        self.used += count
        assert self.used <= N_SEM
        return first

    def copy(self, src, dst, device, index=None):
        if index is None:
            index = self.take()
        return pltpu.make_async_remote_copy(
            src_ref=src,
            dst_ref=dst,
            send_sem=self.send.at[index],
            recv_sem=self.recv.at[index],
            device_id=device,
            device_id_type=MESH,
        )


def mod(value, n):
    return lax.rem(value, n)


def loop(count, body):
    def step(i, carry):
        body(i)
        return carry

    lax.fori_loop(0, count, step, 0)


def kernel(
    hid, gain, slot, valid, w_hbm, teach_hbm,
    f_out, grad_out, rows_out,
    w, teach, f, ft, sf, zin, z32, t32, ts, tt, natural, column, onehot, logits, trow, st, sa, sb, sc, grad,
    po, ps, cr, poz, psz, crz, tx, rx, ty, ry, tza, tzb, rz, ax, ay, az, t2, r2, tz2, rz2, a2, zz, a2z, yy,
    send, recv, wsem, tsem, osem, relayed,
):
    s = lax.axis_index("seq")
    v = lax.axis_index("vocab")
    z, x = lax.div(s, NX), mod(s, NX)
    y, c = lax.div(v, NC), mod(v, NC)
    links = Links(send, recv)

    def at_s(other):
        return (other, v)

    def at_v(other):
        return (s, other)

    def at_z(other):
        return (other * NX + x, v)

    def at_x(other):
        return (z * NX + other, v)

    def at_y(other):
        return (s, other * NC + c)

    wcopy = pltpu.make_async_copy(w_hbm, w, wsem)
    tcopy = pltpu.make_async_copy(teach_hbm, teach, tsem)
    tcopy.start()
    barrier = pltpu.get_barrier_semaphore()

    def greet_vocab(k):
        pl.semaphore_signal(barrier, inc=1, device_id=at_v(mod(v + k + 1, NV)), device_id_type=MESH)

    def greet_z(k):
        pl.semaphore_signal(barrier, inc=1, device_id=at_z(mod(z + k + 1, NZ)), device_id_type=MESH)

    def greet_x(k):
        pl.semaphore_signal(barrier, inc=1, device_id=at_x(mod(x + k + 1, NX)), device_id_type=MESH)

    loop(NX - 1, greet_x)
    loop(NZ - 1, greet_z)
    loop(NV - 1, greet_vocab)
    wcopy.start()

    h = hid[...].astype(F32)
    inv_rms = lax.rsqrt(jnp.mean(h * h, axis=1, keepdims=True) + epsilon)
    for b in range(NV):
        part = h[:, b * CB:(b + 1) * CB] * inv_rms * gain[:, b * CB:(b + 1) * CB]
        for i in range(2):
            sf[i * NV + b:i * NV + b + 1, :] = part[i:i + 1, :]
    zin[z] = sf[...].astype(BF16)
    pl.semaphore_wait(barrier, NX - 1 + NZ - 1 + NV - 1)

    z_first = links.take(NZ)
    teach_first = links.take(NS)

    def z_copy(k):
        return links.copy(zin.at[z], zin.at[z], at_z(mod(z + k, NZ)), z_first + k)

    def z_arrival(k):
        source = mod(z + NZ - k, NZ)
        return links.copy(zin.at[source], zin.at[source], at_z(source), z_first + k)

    def z_pair(i):
        z_copy(4 - i).start()
        z_copy(4 + i).start()

    z_copy(4).start()
    loop(3, lambda i: z_pair(i + 1))

    def relay(k):
        pl.semaphore_signal(relayed, inc=1, device_id=at_x(mod(x + k + 1, NX)), device_id_type=MESH)

    loop(NX - 1, relay)

    def teach_copy(k):
        to = mod(s + k, NS)
        return links.copy(ts.at[to], tt.at[s], at_s(to), teach_first + k)

    def teach_arrival(k):
        source = mod(s + NS - k, NS)
        return links.copy(ts.at[source], tt.at[source], at_s(source), teach_first + k)

    def teach_pair(i):
        teach_copy(i + 1).start()
        teach_copy(NS - 1 - i).start()

    tcopy.wait()
    for b in range(4):
        t32[b] = teach[:, b * 128:(b + 1) * 128].astype(F32)

    def arrange(d):
        for b in range(4):
            ts[d, :, b * 128:(b + 1) * 128] = t32[b, pl.ds(d, 32, stride=NS), :].astype(BF16)

    loop(NS, arrange)
    tt[s] = ts[s]
    pl.semaphore_wait(relayed, NX - 1)
    loop(15, teach_pair)
    teach_copy(NS // 2).start()

    loop(NZ - 1, lambda k: z_arrival(k + 1).wait_recv())
    for b in range(CB // 128):
        z32[b] = zin[:, :, b * 128:(b + 1) * 128].astype(F32).reshape(NZ * 16, 128)
    for b in range(NV):
        for k in range(CB // 128):
            f[c, y, b, x, :, k * 128:(k + 1) * 128] = z32[k, pl.ds(b, 16, stride=NV), :].astype(BF16)

    offsets = (0, 1, 3, 2)
    other_core = (s, y * NC + (1 - c))
    pending, flushes = [], []

    def go(copy):
        copy.start()
        pending.append(copy)

    class Path:
        def __init__(self, span, x_last):
            self.span, self.x_last = span, x_last
            self.cut = (span[0] + span[1] + 1) // 2
            self.a, self.b = (y, x) if x_last else (x, y)
            self.to_a, self.to_b = (at_y, at_x) if x_last else (at_x, at_y)
            self.parts = [mod(self.a + 4 - o, 4) for o in offsets]
            self.up, self.down, self.far = mod(self.b + 1, 4), mod(self.b + 3, 4), mod(self.b + 2, 4)
            self.a_first, self.b_first, self.core_first = links.take(4), links.take(16), links.take(4)

        def ref(self, a, b, low=None, high=None):
            ya, xa = (a, b) if self.x_last else (b, a)
            low = self.span[0] if low is None else low
            high = self.span[1] if high is None else high
            return f.at[c, ya, low:high, xa]

        def a_copy(self, o, part):
            ref = self.ref(part, self.b)
            return links.copy(ref, ref, self.to_a(mod(self.a + o, 4)), self.a_first + o)

        def b_copy(self, kind, i, b, to, low=None, high=None):
            ref = self.ref(self.parts[i], b, low, high)
            return links.copy(ref, ref, self.to_b(to), self.b_first + kind * 4 + i)

        def own(self, i):
            go(self.b_copy(0, i, self.b, self.up))
            go(self.b_copy(1, i, self.b, self.down))

        def forward(self, i):
            self.b_copy(0, i, self.down, self.up).wait_recv()
            go(self.b_copy(2, i, self.down, self.up, None, self.cut))
            self.b_copy(1, i, self.up, self.down).wait_recv()
            go(self.b_copy(3, i, self.up, self.down, self.cut, None))

        def last(self, i):
            self.b_copy(2, i, self.far, self.up, None, self.cut).wait_recv()
            self.b_copy(3, i, self.far, self.down, self.cut, None).wait_recv()

        def core(self, rank, mine):
            b = (self.b, self.down, self.up, self.far)[rank]
            k = c if mine else 1 - c
            low, high = self.span
            ref = f.at[k, :, low:high, b] if self.x_last else f.at[k, b, low:high]
            return links.copy(ref, ref, other_core, self.core_first + rank)

    paths = (Path((0, SPLIT), False), Path((SPLIT, NV), True))
    for path in paths:
        for o in (1, 3, 2):
            go(path.a_copy(o, path.a))
    for path in paths:
        path.own(0)

    quantity = lax.broadcasted_iota(jnp.int32, (128, ROWS), 0)
    natural[...] = jnp.where(quantity == 0, slot[...].astype(F32), valid[...].astype(F32)).T
    for k in range(NC * NY * NX * 2):
        kc, ky, kx, ki = k // 32, k // 8 % 4, k // 2 % 4, k % 2
        column[pl.ds(kc * 256 + ky * 64 + kx * 16 + ki, NZ, stride=2), :] = natural[
            pl.ds(kx * 16 + ky * 4 + kc * 2 + ki, NZ, stride=64), :]

    lane = lax.broadcasted_iota(jnp.int32, (ROWS, 128), 1).astype(F32)
    for b in range(8):
        onehot[:, b * 128:(b + 1) * 128] = jnp.where(column[:, 0:1] == lane + float(b * 128), 1.0, 0.0).astype(BF16)

    for i, o in enumerate(offsets):
        if o:
            for path in paths:
                path.a_copy(o, path.parts[i]).wait_recv()
                path.own(i)
    for path in paths:
        go(path.core(0, True))
    for i in range(4):
        for path in paths:
            path.forward(i)
    for path in paths:
        go(path.core(1, True))
        go(path.core(2, True))
    wcopy.wait()

    def multiply(half):
        logits[half] = jnp.zeros((HALF, COLS), F32)

        def block(b):
            fb = f[half, :, b].reshape(HALF, CB)
            wb = w[pl.ds(b * 5, 5)].reshape(CB, COLS)
            logits[half] += jnp.dot(fb, wb, preferred_element_type=F32)

        loop(NV, block)

    for path in paths:
        for i in range(4):
            path.last(i)
        go(path.core(3, True))
    multiply(c)
    for path in paths:
        for rank in range(4):
            path.core(rank, False).wait_recv()
    multiply(1 - c)

    loop(NS - 1, lambda k: teach_arrival(k + 1).wait_recv())

    def select(i):
        span = pl.ds(pl.multiple_of(i * 256, 256), 256)
        trow[i] = jnp.dot(onehot[span, :], tt[...].reshape(1024, COLS), preferred_element_type=F32)

    loop(2, select)

    def statistics(i):
        span = pl.ds(pl.multiple_of(i * 64, 64), 64)
        inner = pl.ds(pl.multiple_of(mod(i, 4) * 64, 64), 64)
        lo, te = logits[lax.div(i, 4), inner, :], trow[lax.div(i, 4), inner, :]
        top = jnp.max(lo, axis=1, keepdims=True)
        teacher_top = jnp.max(te, axis=1, keepdims=True)
        e = jnp.exp(lo - top)
        total = jnp.sum(e, axis=1, keepdims=True)
        cross = jnp.sum(e * (lo - te), axis=1, keepdims=True)
        teacher_total = jnp.sum(jnp.exp(te - teacher_top), axis=1, keepdims=True)
        place = lax.broadcasted_iota(jnp.int32, (64, 128), 1)
        packed = jnp.where(place == 0, top, jnp.where(place == 1, teacher_top, jnp.where(place == 2, total, jnp.where(
            place == 3, cross, jnp.where(place == 4, teacher_total, 0.0)))))
        st[span, :] = packed

    loop(8, statistics)

    def merged(ref):
        value = ref[...]
        top = jnp.max(value[:, 0:1, :], axis=0, keepdims=True)
        teacher_top = jnp.max(value[:, 1:2, :], axis=0, keepdims=True)
        scale = jnp.exp(value[:, 0:1, :] - top)
        teacher_scale = jnp.exp(value[:, 1:2, :] - teacher_top)
        total = jnp.sum(value[:, 2:3, :] * scale, axis=0)
        cross = jnp.sum(value[:, 3:4, :] * scale, axis=0)
        teacher_total = jnp.sum(value[:, 4:5, :] * teacher_scale, axis=0)
        return top[0], teacher_top[0], total, cross, teacher_total

    def exchange(buffer, here, count, device, blocks):
        start = links.take(count)

        def out(k):
            return links.copy(buffer.at[here], buffer.at[here], device(mod(here + k, count)), start + k)

        def arrival(k):
            source = mod(here + count - k, count)
            return links.copy(buffer.at[source], buffer.at[source], device(source), start + k)

        loop(count - 1, lambda k: out(k + 1).start())
        for b in blocks:
            ft[b] = f[:, :, b].reshape(ROWS, CB).T
        loop(count - 1, lambda k: arrival(k + 1).wait_recv())
        return lambda: loop(count - 1, lambda k: out(k + 1).wait_send())

    def put(buffer, here, rows):
        for r, row in enumerate(rows):
            buffer[here, r:r + 1, :] = row

    sa[v] = st[...].T[0:8, :]
    flushes.append(exchange(sa, v, NV, at_v, (0, 1, 2)))
    put(sb, x, merged(sa))
    flushes.append(exchange(sb, x, NX, at_x, (3, 4)))
    put(sc, z, merged(sb))
    flushes.append(exchange(sc, z, NZ, at_z, (5, 6, 7)))
    f_copy = pltpu.make_async_copy(ft, f_out, osem.at[0])
    f_copy.start()
    top, teacher_top, total, cross, teacher_total = merged(sc)
    student_lse = top + jnp.log(total)
    teacher_lse = teacher_top + jnp.log(teacher_total)
    divergence = cross / total - student_lse + teacher_lse
    st[...] = jnp.where(quantity == 0, student_lse, jnp.where(quantity == 1, teacher_lse, jnp.where(
        quantity == 2, divergence, 0.0))).T

    def gradient(i):
        span = pl.ds(pl.multiple_of(i * 64, 64), 64)
        inner = pl.ds(pl.multiple_of(mod(i, 4) * 64, 64), 64)
        lo, te, q = logits[lax.div(i, 4), inner, :], trow[lax.div(i, 4), inner, :], st[span, :]
        shifted = lo - q[:, 0:1]
        gap = shifted - (te - q[:, 1:2])
        grad[span, :] = (column[span, 1:2] * jnp.exp(shifted) * (gap - q[:, 2:3])).astype(BF16)

    loop(8, gradient)
    grad_copy = pltpu.make_async_copy(grad, grad_out, osem.at[1])
    grad_copy.start()

    def partial(j, half, ref):
        g = grad[pl.ds(pl.multiple_of(half * HALF, HALF), HALF), :]
        if j == 4:
            at = lax.broadcasted_iota(jnp.int32, (HALF, HALF), 0)
            source = (at // 2 % 4) * 64 + (at // 8 % 4) * 16 + (at // 32) * 2 + at % 2
            move = jnp.where(source == lax.broadcasted_iota(jnp.int32, (HALF, HALF), 1), 1.0, 0.0).astype(BF16)
            g = jnp.dot(move, g, preferred_element_type=F32).astype(BF16)
        for n in range(2):
            wn = w[j * 8 + n * 4:j * 8 + n * 4 + 4].reshape(512, COLS)
            product = lax.dot_general(g, wn, (((1,), (1,)), ((), ())), preferred_element_type=F32)
            if j == 4:
                ref[:, :, :, n * 512:(n + 1) * 512] = product.reshape(NZ, NX, 8, 512)
            else:
                ref[j, :, :, :, n * 512:(n + 1) * 512] = product.reshape(NY, NX, 16, 512)

    def add_core(j):
        def step(i):
            if j == 4:
                psz[i] += crz[i]
            else:
                ps[j, i] += cr[j, i]

        loop(NZ if j == 4 else NY, step)

    class Ring:
        def __init__(self, here, device, block, tmp, arrived):
            self.block, self.tmp, self.arrived, self.here = block, tmp, arrived, here
            up, down, far = mod(here + 1, 4), mod(here + 3, 4), mod(here + 2, 4)
            self.up, self.down = up, down
            self.far0 = links.copy(block(far, 0), tmp.at[0], device(up))
            self.far1 = links.copy(block(far, 1), tmp.at[1], device(down))
            self.free0 = links.copy(block(up, 1), arrived.at[0, 1], device(up))
            self.free1 = links.copy(block(down, 0), arrived.at[1, 0], device(down))
            self.last0 = links.copy(tmp.at[0], arrived.at[0, 0], device(up))
            self.last1 = links.copy(tmp.at[1], arrived.at[1, 1], device(down))
            for copy in (self.far0, self.far1, self.free0, self.free1):
                go(copy)

        def middle(self):
            self.far0.wait_recv()
            self.tmp[0] = self.tmp[0] + self.block(self.up, 0)[...]
            go(self.last0)
            self.far1.wait_recv()
            self.tmp[1] = self.tmp[1] + self.block(self.down, 1)[...]
            go(self.last1)

        def finish(self):
            for copy in (self.free0, self.free1, self.last0, self.last1):
                copy.wait_recv()
            return [self.block(self.here, i)[...] + self.arrived[0, i] + self.arrived[1, i] for i in (0, 1)]

    core_links = {j: links.copy(poz, crz, other_core) if j == 4 else links.copy(po.at[j], cr.at[j], other_core) for j in ORDER}
    stage1 = {}

    class Line:
        def __init__(self):
            p = [mod(z + k, NZ) for k in range(NZ)]
            self.p = p
            self.near = [links.copy(psz.at[p[1]], rz.at[0], at_z(p[1])), links.copy(psz.at[p[7]], rz.at[1], at_z(p[7]))]
            self.far = [
                links.copy(psz.at[p[3]], tza.at[0], at_z(p[1])),
                links.copy(psz.at[p[5]], tza.at[1], at_z(p[7])),
                links.copy(psz.at[p[4], 0:2], tzb.at[0], at_z(p[2])),
                links.copy(psz.at[p[4], 2:4], tzb.at[1], at_z(p[6])),
            ]
            self.summed = [links.copy(tza.at[0], rz.at[2], at_z(p[2])), links.copy(tza.at[1], rz.at[3], at_z(p[6]))]
            for copy in self.far + self.near:
                go(copy)

        def middle(self):
            for i, k in ((0, 2), (1, 6)):
                self.far[i].wait_recv()
                self.far[i + 2].wait_recv()
                tza[i] += psz[self.p[k]]
                tza[i, 2 * i:2 * i + 2] += tzb[i]
                go(self.summed[i])

        def finish(self):
            for copy in self.near + self.summed:
                copy.wait_recv()
            az[...] = psz[z] + rz[0] + rz[1] + rz[2] + rz[3]

    def begin(j):
        core_links[j].wait_recv()
        add_core(j)
        if j in XFIRST:
            stage1[j] = Ring(x, at_x, lambda i, half, j=j: ps.at[j, half * 2:half * 2 + 2, i], tx.at[j], rx.at[j])
        elif j in YFIRST:
            stage1[j] = Ring(y, at_y, lambda i, half, j=j: ps.at[j, i, half * 2:half * 2 + 2], ty.at[j - 2], ry.at[j - 2])
        else:
            stage1[j] = Line()

    for n, j in enumerate(ORDER):
        partial(j, 1 - c, poz if j == 4 else po)
        go(core_links[j])
        partial(j, c, psz if j == 4 else ps)
        if n:
            begin(ORDER[n - 1])
    begin(ORDER[-1])

    for j in (0, 2, 4, 1, 3):
        stage1[j].middle()

    def spread(buffer, source, here, count, device):
        start = links.take(count)

        def out(k):
            to = mod(here + k, count)
            return links.copy(source.at[to], buffer.at[here], device(to), start + k)

        def arrival(k):
            other = mod(here + count - k, count)
            return links.copy(source.at[other], buffer.at[other], device(other), start + k)

        loop(count - 1, lambda k: out(k + 1).start())
        buffer[here] = source[here]
        flushes.append(lambda: loop(count - 1, lambda k: out(k + 1).wait_send()))
        return lambda: loop(count - 1, lambda k: arrival(k + 1).wait_recv())

    stage2, stage3 = {}, {}
    for j in (0, 2, 1, 3, 4):
        if j == 4:
            stage1[4].finish()
            stage2[4] = Ring(x, at_x, lambda i, half: az.at[i, :, half * 512:half * 512 + 512], tz2, rz2)
            continue
        low, high = stage1[j].finish()
        mine = ax.at[j] if j in XFIRST else ay.at[j - 2]
        mine[0:2] = low
        mine[2:4] = high
        here, device = (y, at_y) if j in XFIRST else (x, at_x)
        stage2[j] = Ring(here, device, lambda i, half, m=mine: m.at[i, half * 8:half * 8 + 8], t2.at[j], r2.at[j])
    for j in (0, 2, 1, 3, 4):
        stage2[j].middle()
    for j in (0, 2, 1, 3, 4):
        low, high = stage2[j].finish()
        if j == 4:
            for k in range(NY):
                a2z[k, :, 0:512] = low[2 * k:2 * k + 2, :]
                a2z[k, :, 512:1024] = high[2 * k:2 * k + 2, :]
            stage3[j] = spread(yy, a2z, y, NY, at_y)
        else:
            for k in range(4):
                a2[j, k] = low[2 * k:2 * k + 2, :]
                a2[j, k + 4] = high[2 * k:2 * k + 2, :]
            stage3[j] = spread(zz.at[j], a2.at[j], z, NZ, at_z)
    for j in (0, 2, 1, 3, 4):
        stage3[j]()
        arrived = yy[...] if j == 4 else zz[j]
        rows_out[j] = jnp.sum(arrived, axis=0)

    f_copy.wait()
    grad_copy.wait()
    for copy in pending:
        copy.wait_send()
    loop(NZ - 1, lambda k: z_copy(k + 1).wait_send())
    loop(NS - 1, lambda k: teach_copy(k + 1).wait_send())
    for flush in flushes:
        flush()


def finish_kernel(hid, gain, rows, f_hbm, grad_hbm, gh_out, head_hbm, f, grad, stage, gsem, fsem, osem):
    gcopy = pltpu.make_async_copy(grad_hbm, grad, gsem)
    gcopy.start()
    fcopies = [pltpu.make_async_copy(f_hbm.at[b], f.at[b], fsem.at[b]) for b in range(NV)]
    ocopies = [pltpu.make_async_copy(stage.at[b], head_hbm.at[b], osem.at[b]) for b in range(NV)]
    for copy in fcopies:
        copy.start()
    h = hid[...].astype(F32)
    inv_rms = lax.rsqrt(jnp.mean(h * h, axis=1, keepdims=True) + epsilon)
    dots = jnp.zeros((2, 1), F32)
    for j in range(NJ):
        span = slice(j * SB, (j + 1) * SB)
        dots = dots + jnp.sum(rows[j] * gain[:, span] * (h[:, span] * inv_rms), axis=1, keepdims=True)
    dots = dots / D
    for j in range(NJ):
        span = slice(j * SB, (j + 1) * SB)
        gh_out[:, span] = (inv_rms * (rows[j] * gain[:, span] - h[:, span] * inv_rms * dots)).astype(BF16)
    gcopy.wait()
    for b in range(NV):
        fcopies[b].wait()
        stage[b] = jnp.dot(f[b], grad[...], preferred_element_type=F32).astype(BF16)
        ocopies[b].start()
    for copy in ocopies:
        copy.wait()


def shards(hidden, norm_gain, head_weight, teacher_logits, teacher_slot, valid_tokens):
    vmem = pl.BlockSpec(memory_space=pltpu.VMEM)
    hbm = pl.BlockSpec(memory_space=pl.ANY)
    scratch = [
        pltpu.VMEM((40, 128, COLS), BF16),
        pltpu.VMEM((1024, COLS), BF16),
        pltpu.VMEM((NC, NY, NV, NX, 16, CB), BF16),
        pltpu.VMEM((NV, CB, ROWS), BF16),
        pltpu.VMEM((16, CB), F32),
        pltpu.VMEM((NZ, 16, CB), BF16),
        pltpu.VMEM((5, 128, 128), F32),
        pltpu.VMEM((4, 1024, 128), F32),
        pltpu.VMEM((NS, 32, COLS), BF16),
        pltpu.VMEM((NS, 32, COLS), BF16),
        pltpu.VMEM((ROWS, 128), F32),
        pltpu.VMEM((ROWS, 128), F32),
        pltpu.VMEM((ROWS, 1024), BF16),
        pltpu.VMEM((NC, HALF, COLS), F32),
        pltpu.VMEM((NC, HALF, COLS), F32),
        pltpu.VMEM((ROWS, 128), F32),
        pltpu.VMEM((NV, 8, ROWS), F32),
        pltpu.VMEM((NX, 8, ROWS), F32),
        pltpu.VMEM((NZ, 8, ROWS), F32),
        pltpu.VMEM((ROWS, COLS), BF16),
        pltpu.VMEM((4, NY, NX, 16, SB), F32),
        pltpu.VMEM((4, NY, NX, 16, SB), F32),
        pltpu.VMEM((4, NY, NX, 16, SB), F32),
        pltpu.VMEM((NZ, NX, 8, SB), F32),
        pltpu.VMEM((NZ, NX, 8, SB), F32),
        pltpu.VMEM((NZ, NX, 8, SB), F32),
        pltpu.VMEM((2, 2, 2, 16, SB), F32),
        pltpu.VMEM((2, 2, 2, 2, 16, SB), F32),
        pltpu.VMEM((2, 2, 2, 16, SB), F32),
        pltpu.VMEM((2, 2, 2, 2, 16, SB), F32),
        pltpu.VMEM((2, NX, 8, SB), F32),
        pltpu.VMEM((2, 2, 8, SB), F32),
        pltpu.VMEM((4, NX, 8, SB), F32),
        pltpu.VMEM((2, NY, 16, SB), F32),
        pltpu.VMEM((2, NX, 16, SB), F32),
        pltpu.VMEM((NX, 8, SB), F32),
        pltpu.VMEM((4, 2, 8, SB), F32),
        pltpu.VMEM((4, 2, 2, 8, SB), F32),
        pltpu.VMEM((2, 8, SB // 2), F32),
        pltpu.VMEM((2, 2, 8, SB // 2), F32),
        pltpu.VMEM((4, NZ, 2, SB), F32),
        pltpu.VMEM((4, NZ, 2, SB), F32),
        pltpu.VMEM((NY, 2, SB), F32),
        pltpu.VMEM((NY, 2, SB), F32),
        pltpu.SemaphoreType.DMA((N_SEM,)),
        pltpu.SemaphoreType.DMA((N_SEM,)),
        pltpu.SemaphoreType.DMA,
        pltpu.SemaphoreType.DMA,
        pltpu.SemaphoreType.DMA((2,)),
        pltpu.SemaphoreType.REGULAR,
    ]
    gain = norm_gain.reshape(1, D)
    features, grad, rows = pl.pallas_call(
        kernel,
        out_shape=(
            jax.ShapeDtypeStruct((NV, CB, ROWS), BF16),
            jax.ShapeDtypeStruct((ROWS, COLS), BF16),
            jax.ShapeDtypeStruct((NJ, 2, SB), F32),
        ),
        in_specs=[vmem, vmem, vmem, vmem, hbm, hbm],
        out_specs=(hbm, hbm, vmem),
        scratch_shapes=scratch,
        compiler_params=pltpu.CompilerParams(
            collective_id=0, has_side_effects=True, vmem_limit_bytes=60 * 2**20
        ),
        name="distill_head",
    )(
        hidden,
        gain,
        teacher_slot.reshape(1, ROWS),
        valid_tokens.reshape(1, ROWS),
        head_weight.reshape(40, 128, COLS),
        teacher_logits.reshape(1024, COLS),
    )

    grad_hidden, grad_head = pl.pallas_call(
        finish_kernel,
        out_shape=(jax.ShapeDtypeStruct((2, D), BF16), jax.ShapeDtypeStruct((NV, CB, COLS), BF16)),
        in_specs=[vmem, vmem, vmem, hbm, hbm],
        out_specs=(vmem, hbm),
        scratch_shapes=[
            pltpu.VMEM((NV, CB, ROWS), BF16),
            pltpu.VMEM((ROWS, COLS), BF16),
            pltpu.VMEM((NV, CB, COLS), BF16),
            pltpu.SemaphoreType.DMA,
            pltpu.SemaphoreType.DMA((NV,)),
            pltpu.SemaphoreType.DMA((NV,)),
        ],
        compiler_params=pltpu.CompilerParams(vmem_limit_bytes=60 * 2**20),
        name="head_gradient",
    )(hidden, gain, rows, features, grad)
    return grad_hidden, grad_head.reshape(D, COLS)


def solution(mesh):
    placed = (
        P(("seq", "vocab"), None),
        P(),
        P(None, ("seq", "vocab")),
        P("seq", None, "vocab"),
        P(),
        P(),
    )
    return jax.shard_map(
        shards,
        mesh=mesh,
        in_specs=placed,
        out_specs=(P(("seq", "vocab"), None), P(None, ("seq", "vocab"))),
        check_vma=False,
    )
```

```python
import functools

import jax
import jax.numpy as jnp
from jax import lax
from jax.experimental import pallas as pl
from jax.experimental.pallas import tpu as pltpu
from jax.sharding import PartitionSpec as P

MESH = pl.DeviceIdType.MESH
F32 = jnp.float32
BF16 = jnp.bfloat16
epsilon = 1e-06

NZ, NX, NY, NC = 8, 4, 4, 2
NV, NS = NY * NC, NZ * NX
ROWS, D, CB, SB, COLS = 512, 5120, 640, 1024, 512
HALF = ROWS // NC
NJ = 5
ORDER = (4, 0, 2, 1, 3)
XFIRST, YFIRST = (0, 1), (2, 3)
N_SEM = 240
LIMIT = 55
FIRST = 7
SPLIT = 6


class Links:
    def __init__(self, send, recv):
        self.send, self.recv, self.used = send, recv, 0

    def take(self, count=1):
        first = self.used
        self.used += count
        assert self.used <= N_SEM
        return first

    def copy(self, src, dst, device, index=None):
        if index is None:
            index = self.take()
        return pltpu.make_async_remote_copy(
            src_ref=src,
            dst_ref=dst,
            send_sem=self.send.at[index],
            recv_sem=self.recv.at[index],
            device_id=device,
            device_id_type=MESH,
        )


def mod(value, n):
    return lax.rem(value, n)


def loop(count, body):
    def step(i, carry):
        body(i)
        return carry

    lax.fori_loop(0, count, step, 0)


def kernel(
    hid_hbm, gain_hbm, slot_hbm, valid_hbm, w_hbm, teach_hbm,
    ft, grad, rows,
    hid, gain, slot, valid, w, teach, f, sf, zin, z32, t32, ts, tt, natural, column, onehot, logits, trow, st, sa, sb, sc,
    po, ps, cr, poz, psz, crz, tx, rx, ty, ry, tza, tzb, rz, ax, ay, az, t2, r2, tz2, rz2, a2, zz, a2z, yy,
    send, recv, isem, wsem, tsem, relayed,
):
    s = lax.axis_index("seq")
    v = lax.axis_index("vocab")
    z, x = lax.div(s, NX), mod(s, NX)
    y, c = lax.div(v, NC), mod(v, NC)
    links = Links(send, recv)

    def at_s(other):
        return (other, v)

    def at_v(other):
        return (s, other)

    def at_z(other):
        return (other * NX + x, v)

    def at_x(other):
        return (z * NX + other, v)

    def at_y(other):
        return (s, other * NC + c)

    wcopy = pltpu.make_async_copy(w_hbm, w, wsem)
    tcopy = pltpu.make_async_copy(teach_hbm, teach, tsem)
    inputs = [
        pltpu.make_async_copy(source, target, isem.at[i])
        for i, (source, target) in enumerate(((hid_hbm, hid), (gain_hbm, gain), (slot_hbm, slot), (valid_hbm, valid)))
    ]
    for copy in inputs:
        copy.start()
    tcopy.start()
    barrier = pltpu.get_barrier_semaphore()

    def greet_vocab(k):
        pl.semaphore_signal(barrier, inc=1, device_id=at_v(mod(v + k + 1, NV)), device_id_type=MESH)

    def greet_z(k):
        pl.semaphore_signal(barrier, inc=1, device_id=at_z(mod(z + k + 1, NZ)), device_id_type=MESH)

    def greet_x(k):
        pl.semaphore_signal(barrier, inc=1, device_id=at_x(mod(x + k + 1, NX)), device_id_type=MESH)

    loop(NX - 1, greet_x)
    loop(NZ - 1, greet_z)
    loop(NV - 1, greet_vocab)
    wcopy.start()

    for copy in inputs:
        copy.wait()
    h = hid[...].astype(F32)
    inv_rms = lax.rsqrt(jnp.mean(h * h, axis=1, keepdims=True) + epsilon)
    for b in range(NV):
        part = h[:, b * CB:(b + 1) * CB] * inv_rms * gain[:, b * CB:(b + 1) * CB]
        for i in range(2):
            sf[i * NV + b:i * NV + b + 1, :] = part[i:i + 1, :]
    zin[z] = sf[...].astype(BF16)
    pl.semaphore_wait(barrier, NX - 1 + NZ - 1 + NV - 1)

    z_first = links.take(NZ)
    teach_first = links.take(NS)

    def z_copy(k):
        return links.copy(zin.at[z], zin.at[z], at_z(mod(z + k, NZ)), z_first + k)

    def z_arrival(k):
        source = mod(z + NZ - k, NZ)
        return links.copy(zin.at[source], zin.at[source], at_z(source), z_first + k)

    def z_pair(i):
        z_copy(4 - i).start()
        z_copy(4 + i).start()

    z_copy(4).start()
    loop(3, lambda i: z_pair(i + 1))

    def relay(k):
        pl.semaphore_signal(relayed, inc=1, device_id=at_x(mod(x + k + 1, NX)), device_id_type=MESH)

    loop(NX - 1, relay)

    def teach_copy(dz, dx):
        to = mod(z + dz, NZ) * NX + mod(x + dx, NX)
        return links.copy(ts.at[to], tt.at[s], at_s(to), teach_first + dz * NX + dx)

    def teach_arrival(dz, dx):
        source = mod(z + NZ - dz, NZ) * NX + mod(x + NX - dx, NX)
        return links.copy(ts.at[source], tt.at[source], at_s(source), teach_first + dz * NX + dx)

    teach_order = [(dz, dx) for dx in (0, 1, 3, 2) for dz in (0, 1, 7, 2, 6, 3, 5, 4) if dz or dx]

    tcopy.wait()
    for b in range(4):
        t32[b] = teach[:, b * 128:(b + 1) * 128].astype(F32)

    def arrange(d):
        for b in range(4):
            ts[d, :, b * 128:(b + 1) * 128] = t32[b, pl.ds(d, 32, stride=NS), :].astype(BF16)

    loop(NS, arrange)
    tt[s] = ts[s]
    pl.semaphore_wait(relayed, NX - 1)
    for dz, dx in teach_order[:FIRST]:
        teach_copy(dz, dx).start()

    loop(NZ - 1, lambda k: z_arrival(k + 1).wait_recv())
    for b in range(CB // 128):
        z32[b] = zin[:, :, b * 128:(b + 1) * 128].astype(F32).reshape(NZ * 16, 128)
    for b in range(NV):
        for k in range(CB // 128):
            f[c, y, b, x, :, k * 128:(k + 1) * 128] = z32[k, pl.ds(b, 16, stride=NV), :].astype(BF16)

    offsets = (0, 1, 3, 2)
    other_core = (s, y * NC + (1 - c))
    pending, flushes = [], []

    def go(copy):
        copy.start()
        pending.append(copy)

    class Path:
        def __init__(self, span, x_last):
            self.span, self.x_last = span, x_last
            self.cut = (span[0] + span[1] + 1) // 2
            self.a, self.b = (y, x) if x_last else (x, y)
            self.to_a, self.to_b = (at_y, at_x) if x_last else (at_x, at_y)
            self.parts = [mod(self.a + 4 - o, 4) for o in offsets]
            self.up, self.down, self.far = mod(self.b + 1, 4), mod(self.b + 3, 4), mod(self.b + 2, 4)
            self.a_first, self.b_first, self.core_first = links.take(4), links.take(16), links.take(4)

        def ref(self, a, b, low=None, high=None):
            ya, xa = (a, b) if self.x_last else (b, a)
            low = self.span[0] if low is None else low
            high = self.span[1] if high is None else high
            return f.at[c, ya, low:high, xa]

        def a_copy(self, o, part):
            ref = self.ref(part, self.b)
            return links.copy(ref, ref, self.to_a(mod(self.a + o, 4)), self.a_first + o)

        def b_copy(self, kind, i, b, to, low=None, high=None):
            ref = self.ref(self.parts[i], b, low, high)
            return links.copy(ref, ref, self.to_b(to), self.b_first + kind * 4 + i)

        def own(self, i):
            go(self.b_copy(0, i, self.b, self.up))
            go(self.b_copy(1, i, self.b, self.down))

        def forward(self, i):
            self.b_copy(0, i, self.down, self.up).wait_recv()
            go(self.b_copy(2, i, self.down, self.up, None, self.cut))
            self.b_copy(1, i, self.up, self.down).wait_recv()
            go(self.b_copy(3, i, self.up, self.down, self.cut, None))

        def last(self, i):
            self.b_copy(2, i, self.far, self.up, None, self.cut).wait_recv()
            self.b_copy(3, i, self.far, self.down, self.cut, None).wait_recv()

        def core(self, rank, mine):
            b = (self.b, self.down, self.up, self.far)[rank]
            k = c if mine else 1 - c
            low, high = self.span
            ref = f.at[k, :, low:high, b] if self.x_last else f.at[k, b, low:high]
            return links.copy(ref, ref, other_core, self.core_first + rank)

    paths = (Path((0, SPLIT), False), Path((SPLIT, NV), True))
    for path in paths:
        for o in (1, 3, 2):
            go(path.a_copy(o, path.a))
    for path in paths:
        path.own(0)

    for dz, dx in teach_order[FIRST:]:
        teach_copy(dz, dx).start()

    quantity = lax.broadcasted_iota(jnp.int32, (128, ROWS), 0)
    natural[...] = jnp.where(quantity == 0, slot[...].astype(F32), valid[...].astype(F32)).T
    for k in range(NC * NY * NX * 2):
        kc, ky, kx, ki = k // 32, k // 8 % 4, k // 2 % 4, k % 2
        column[pl.ds(kc * 256 + ky * 64 + kx * 16 + ki, NZ, stride=2), :] = natural[
            pl.ds(kx * 16 + ky * 4 + kc * 2 + ki, NZ, stride=64), :]

    lane = lax.broadcasted_iota(jnp.int32, (ROWS, 128), 1).astype(F32)
    for b in range(8):
        onehot[:, b * 128:(b + 1) * 128] = jnp.where(column[:, 0:1] == lane + float(b * 128), 1.0, 0.0).astype(BF16)

    for i, o in enumerate(offsets):
        if o:
            for path in paths:
                path.a_copy(o, path.parts[i]).wait_recv()
                path.own(i)
    for path in paths:
        go(path.core(0, True))
    for i in range(4):
        for path in paths:
            path.forward(i)
    for path in paths:
        go(path.core(1, True))
        go(path.core(2, True))
    wcopy.wait()

    def multiply(half):
        logits[half] = jnp.zeros((HALF, COLS), F32)

        def block(b):
            fb = f[half, :, b].reshape(HALF, CB)
            wb = w[pl.ds(b * 5, 5)].reshape(CB, COLS)
            logits[half] += jnp.dot(fb, wb, preferred_element_type=F32)

        loop(NV, block)

    for path in paths:
        for i in range(4):
            path.last(i)
        go(path.core(3, True))
    multiply(c)
    for path in paths:
        for rank in range(4):
            path.core(rank, False).wait_recv()
    multiply(1 - c)

    for dz, dx in teach_order:
        teach_arrival(dz, dx).wait_recv()

    def select(i):
        span = pl.ds(pl.multiple_of(i * 256, 256), 256)
        trow[i] = jnp.dot(onehot[span, :], tt[...].reshape(1024, COLS), preferred_element_type=F32)

    loop(2, select)

    def statistics(i):
        span = pl.ds(pl.multiple_of(i * 64, 64), 64)
        inner = pl.ds(pl.multiple_of(mod(i, 4) * 64, 64), 64)
        lo, te = logits[lax.div(i, 4), inner, :], trow[lax.div(i, 4), inner, :]
        top = jnp.max(lo, axis=1, keepdims=True)
        teacher_top = jnp.max(te, axis=1, keepdims=True)
        e = jnp.exp(lo - top)
        total = jnp.sum(e, axis=1, keepdims=True)
        cross = jnp.sum(e * (lo - te), axis=1, keepdims=True)
        teacher_total = jnp.sum(jnp.exp(te - teacher_top), axis=1, keepdims=True)
        place = lax.broadcasted_iota(jnp.int32, (64, 128), 1)
        packed = jnp.where(place == 0, top + jnp.log(total), jnp.where(
            place == 1, teacher_top + jnp.log(teacher_total), jnp.where(place == 2, cross / total, 0.0)))
        st[span, :] = packed

    loop(8, statistics)

    def merged(ref):
        value = ref[...]

        def lse(part):
            top = jnp.max(part, axis=0)
            scale = jnp.exp(part - top[None])
            total = jnp.sum(scale, axis=0)
            return top + jnp.log(total), scale, total

        student_lse, scale, total = lse(value[:, 0:1, :])
        teacher_lse, _, _ = lse(value[:, 1:2, :])
        return student_lse, teacher_lse, jnp.sum(scale * value[:, 2:3, :], axis=0) / total

    def exchange(buffer, here, count, device, blocks):
        start = links.take(count)

        def out(k):
            return links.copy(buffer.at[here], buffer.at[here], device(mod(here + k, count)), start + k)

        def arrival(k):
            source = mod(here + count - k, count)
            return links.copy(buffer.at[source], buffer.at[source], device(source), start + k)

        loop(count - 1, lambda k: out(k + 1).start())
        for b in blocks:
            ft[b] = f[:, :, b].reshape(ROWS, CB).T
        loop(count - 1, lambda k: arrival(k + 1).wait_recv())
        return lambda: loop(count - 1, lambda k: out(k + 1).wait_send())

    def put(buffer, here, rows):
        for r, row in enumerate(rows):
            buffer[here, r:r + 1, :] = row

    sa[v] = st[...].T[0:4, :]
    flushes.append(exchange(sa, v, NV, at_v, (0, 1, 2)))
    put(sb, x, merged(sa))
    flushes.append(exchange(sb, x, NX, at_x, (3, 4)))
    put(sc, z, merged(sb))
    flushes.append(exchange(sc, z, NZ, at_z, (5, 6, 7)))
    student_lse, teacher_lse, mean_gap = merged(sc)
    divergence = mean_gap - student_lse + teacher_lse
    st[...] = jnp.where(quantity == 0, student_lse, jnp.where(quantity == 1, teacher_lse, jnp.where(
        quantity == 2, divergence, 0.0))).T

    def gradient(i):
        span = pl.ds(pl.multiple_of(i * 64, 64), 64)
        inner = pl.ds(pl.multiple_of(mod(i, 4) * 64, 64), 64)
        lo, te, q = logits[lax.div(i, 4), inner, :], trow[lax.div(i, 4), inner, :], st[span, :]
        shifted = lo - q[:, 0:1]
        gap = shifted - (te - q[:, 1:2])
        grad[span, :] = (column[span, 1:2] * jnp.exp(shifted) * (gap - q[:, 2:3])).astype(BF16)

    loop(8, gradient)

    def partial(j, half, ref):
        g = grad[pl.ds(pl.multiple_of(half * HALF, HALF), HALF), :]
        if j == 4:
            at = lax.broadcasted_iota(jnp.int32, (HALF, HALF), 0)
            source = (at // 2 % 4) * 64 + (at // 8 % 4) * 16 + (at // 32) * 2 + at % 2
            move = jnp.where(source == lax.broadcasted_iota(jnp.int32, (HALF, HALF), 1), 1.0, 0.0).astype(BF16)
            g = jnp.dot(move, g, preferred_element_type=F32).astype(BF16)
        for n in range(2):
            wn = w[j * 8 + n * 4:j * 8 + n * 4 + 4].reshape(512, COLS)
            product = lax.dot_general(g, wn, (((1,), (1,)), ((), ())), preferred_element_type=F32)
            if j == 4:
                ref[:, :, :, n * 512:(n + 1) * 512] = product.reshape(NZ, NX, 8, 512)
            else:
                ref[j, :, :, :, n * 512:(n + 1) * 512] = product.reshape(NY, NX, 16, 512)

    def add_core(j):
        def step(i):
            if j == 4:
                psz[i] += crz[i]
            else:
                ps[j, i] += cr[j, i]

        loop(NZ if j == 4 else NY, step)

    class Ring:
        def __init__(self, here, device, block, tmp, arrived):
            self.block, self.tmp, self.arrived, self.here = block, tmp, arrived, here
            up, down, far = mod(here + 1, 4), mod(here + 3, 4), mod(here + 2, 4)
            self.up, self.down = up, down
            self.far0 = links.copy(block(far, 0), tmp.at[0], device(up))
            self.far1 = links.copy(block(far, 1), tmp.at[1], device(down))
            self.free0 = links.copy(block(up, 1), arrived.at[0, 1], device(up))
            self.free1 = links.copy(block(down, 0), arrived.at[1, 0], device(down))
            self.last0 = links.copy(tmp.at[0], arrived.at[0, 0], device(up))
            self.last1 = links.copy(tmp.at[1], arrived.at[1, 1], device(down))
            for copy in (self.far0, self.far1, self.free0, self.free1):
                go(copy)

        def middle(self):
            self.far0.wait_recv()
            self.tmp[0] = self.tmp[0] + self.block(self.up, 0)[...]
            go(self.last0)
            self.far1.wait_recv()
            self.tmp[1] = self.tmp[1] + self.block(self.down, 1)[...]
            go(self.last1)

        def finish(self):
            for copy in (self.free0, self.free1, self.last0, self.last1):
                copy.wait_recv()
            return [self.block(self.here, i)[...] + self.arrived[0, i] + self.arrived[1, i] for i in (0, 1)]

    core_links = {j: links.copy(poz, crz, other_core) if j == 4 else links.copy(po.at[j], cr.at[j], other_core) for j in ORDER}
    stage1 = {}

    class Line:
        def __init__(self):
            p = [mod(z + k, NZ) for k in range(NZ)]
            self.p = p
            self.near = [links.copy(psz.at[p[1]], rz.at[0], at_z(p[1])), links.copy(psz.at[p[7]], rz.at[1], at_z(p[7]))]
            self.far = [
                links.copy(psz.at[p[3]], tza.at[0], at_z(p[1])),
                links.copy(psz.at[p[5]], tza.at[1], at_z(p[7])),
                links.copy(psz.at[p[4], 0:2], tzb.at[0], at_z(p[2])),
                links.copy(psz.at[p[4], 2:4], tzb.at[1], at_z(p[6])),
            ]
            self.summed = [links.copy(tza.at[0], rz.at[2], at_z(p[2])), links.copy(tza.at[1], rz.at[3], at_z(p[6]))]
            for copy in self.far + self.near:
                go(copy)

        def middle(self):
            for i, k in ((0, 2), (1, 6)):
                self.far[i].wait_recv()
                self.far[i + 2].wait_recv()
                tza[i] += psz[self.p[k]]
                tza[i, 2 * i:2 * i + 2] += tzb[i]
                go(self.summed[i])

        def finish(self):
            for copy in self.near + self.summed:
                copy.wait_recv()
            az[...] = psz[z] + rz[0] + rz[1] + rz[2] + rz[3]

    def begin(j):
        core_links[j].wait_recv()
        add_core(j)
        if j in XFIRST:
            stage1[j] = Ring(x, at_x, lambda i, half, j=j: ps.at[j, half * 2:half * 2 + 2, i], tx.at[j], rx.at[j])
        elif j in YFIRST:
            stage1[j] = Ring(y, at_y, lambda i, half, j=j: ps.at[j, i, half * 2:half * 2 + 2], ty.at[j - 2], ry.at[j - 2])
        else:
            stage1[j] = Line()

    for n, j in enumerate(ORDER):
        partial(j, 1 - c, poz if j == 4 else po)
        go(core_links[j])
        partial(j, c, psz if j == 4 else ps)
        if n:
            begin(ORDER[n - 1])
    begin(ORDER[-1])

    for j in (0, 2, 4, 1, 3):
        stage1[j].middle()

    def spread(buffer, source, here, count, device):
        start = links.take(count)

        def out(k):
            to = mod(here + k, count)
            return links.copy(source.at[to], buffer.at[here], device(to), start + k)

        def arrival(k):
            other = mod(here + count - k, count)
            return links.copy(source.at[other], buffer.at[other], device(other), start + k)

        loop(count - 1, lambda k: out(k + 1).start())
        buffer[here] = source[here]
        flushes.append(lambda: loop(count - 1, lambda k: out(k + 1).wait_send()))
        return lambda: loop(count - 1, lambda k: arrival(k + 1).wait_recv())

    stage2, stage3 = {}, {}

    def second(j):
        if j == 4:
            stage1[4].finish()
            stage2[4] = Ring(x, at_x, lambda i, half: az.at[i, :, half * 512:half * 512 + 512], tz2, rz2)
            return
        low, high = stage1[j].finish()
        mine = ax.at[j] if j in XFIRST else ay.at[j - 2]
        mine[0:2] = low
        mine[2:4] = high
        here, device = (y, at_y) if j in XFIRST else (x, at_x)
        stage2[j] = Ring(here, device, lambda i, half: mine.at[i, half * 8:half * 8 + 8], t2.at[j], r2.at[j])

    def third(j):
        low, high = stage2[j].finish()
        if j == 4:
            for k in range(NY):
                a2z[k, :, 0:512] = low[2 * k:2 * k + 2, :]
                a2z[k, :, 512:1024] = high[2 * k:2 * k + 2, :]
            stage3[j] = spread(yy, a2z, y, NY, at_y)
        else:
            for k in range(4):
                a2[j, k] = low[2 * k:2 * k + 2, :]
                a2[j, k + 4] = high[2 * k:2 * k + 2, :]
            stage3[j] = spread(zz.at[j], a2.at[j], z, NZ, at_z)

    for j in (0, 2, 1, 3, 4):
        second(j)
    for j in (0, 2, 1, 3, 4):
        stage2[j].middle()
    for j in (0, 2, 1, 3, 4):
        third(j)
    for j in (0, 2, 1, 3, 4):
        stage3[j]()
        rows[j] = jnp.sum(yy[...] if j == 4 else zz[j], axis=0)

    for copy in pending:
        copy.wait_send()
    loop(NZ - 1, lambda k: z_copy(k + 1).wait_send())
    for dz, dx in teach_order:
        teach_copy(dz, dx).wait_send()
    for flush in flushes:
        flush()


def finish_kernel(hid_hbm, gain_hbm, rows, ft, grad, gh_hbm, head_hbm, hid, gain, gh, stage, isem, osem):
    inputs = [pltpu.make_async_copy(hid_hbm, hid, isem.at[0]), pltpu.make_async_copy(gain_hbm, gain, isem.at[1])]
    outputs = [pltpu.make_async_copy(stage.at[b], head_hbm.at[b], osem.at[b]) for b in range(NV)]
    outputs.append(pltpu.make_async_copy(gh, gh_hbm, osem.at[NV]))
    for copy in inputs:
        copy.start()

    def head_block(b):
        stage[b] = jnp.dot(ft[b], grad[...], preferred_element_type=F32).astype(BF16)
        outputs[b].start()

    for b in range(4):
        head_block(b)
    for copy in inputs:
        copy.wait()
    h = hid[...].astype(F32)
    inv_rms = lax.rsqrt(jnp.mean(h * h, axis=1, keepdims=True) + epsilon)
    dots = jnp.zeros((2, 1), F32)
    for j in range(NJ):
        span = slice(j * SB, (j + 1) * SB)
        dots = dots + jnp.sum(rows[j] * gain[:, span] * (h[:, span] * inv_rms), axis=1, keepdims=True)
    dots = dots / D
    for j in range(NJ):
        span = slice(j * SB, (j + 1) * SB)
        gh[:, span] = (inv_rms * (rows[j] * gain[:, span] - h[:, span] * inv_rms * dots)).astype(BF16)
    outputs[NV].start()
    for b in range(4, NV):
        head_block(b)
    for copy in outputs:
        copy.wait()


def shards(hidden, norm_gain, head_weight, teacher_logits, teacher_slot, valid_tokens):
    vmem = pl.BlockSpec(memory_space=pltpu.VMEM)
    hbm = pl.BlockSpec(memory_space=pl.ANY)
    scratch = [
        pltpu.VMEM((2, D), BF16),
        pltpu.VMEM((1, D), F32),
        pltpu.VMEM((1, ROWS), jnp.int32),
        pltpu.VMEM((1, ROWS), jnp.int32),
        pltpu.VMEM((40, 128, COLS), BF16),
        pltpu.VMEM((1024, COLS), BF16),
        pltpu.VMEM((NC, NY, NV, NX, 16, CB), BF16),
        pltpu.VMEM((16, CB), F32),
        pltpu.VMEM((NZ, 16, CB), BF16),
        pltpu.VMEM((5, 128, 128), F32),
        pltpu.VMEM((4, 1024, 128), F32),
        pltpu.VMEM((NS, 32, COLS), BF16),
        pltpu.VMEM((NS, 32, COLS), BF16),
        pltpu.VMEM((ROWS, 128), F32),
        pltpu.VMEM((ROWS, 128), F32),
        pltpu.VMEM((ROWS, 1024), BF16),
        pltpu.VMEM((NC, HALF, COLS), F32),
        pltpu.VMEM((NC, HALF, COLS), F32),
        pltpu.VMEM((ROWS, 128), F32),
        pltpu.VMEM((NV, 4, ROWS), F32),
        pltpu.VMEM((NX, 4, ROWS), F32),
        pltpu.VMEM((NZ, 4, ROWS), F32),
        pltpu.VMEM((4, NY, NX, 16, SB), F32),
        pltpu.VMEM((4, NY, NX, 16, SB), F32),
        pltpu.VMEM((4, NY, NX, 16, SB), F32),
        pltpu.VMEM((NZ, NX, 8, SB), F32),
        pltpu.VMEM((NZ, NX, 8, SB), F32),
        pltpu.VMEM((NZ, NX, 8, SB), F32),
        pltpu.VMEM((2, 2, 2, 16, SB), F32),
        pltpu.VMEM((2, 2, 2, 2, 16, SB), F32),
        pltpu.VMEM((2, 2, 2, 16, SB), F32),
        pltpu.VMEM((2, 2, 2, 2, 16, SB), F32),
        pltpu.VMEM((2, NX, 8, SB), F32),
        pltpu.VMEM((2, 2, 8, SB), F32),
        pltpu.VMEM((4, NX, 8, SB), F32),
        pltpu.VMEM((2, NY, 16, SB), F32),
        pltpu.VMEM((2, NX, 16, SB), F32),
        pltpu.VMEM((NX, 8, SB), F32),
        pltpu.VMEM((4, 2, 8, SB), F32),
        pltpu.VMEM((4, 2, 2, 8, SB), F32),
        pltpu.VMEM((2, 8, SB // 2), F32),
        pltpu.VMEM((2, 2, 8, SB // 2), F32),
        pltpu.VMEM((4, NZ, 2, SB), F32),
        pltpu.VMEM((4, NZ, 2, SB), F32),
        pltpu.VMEM((NY, 2, SB), F32),
        pltpu.VMEM((NY, 2, SB), F32),
        pltpu.SemaphoreType.DMA((N_SEM,)),
        pltpu.SemaphoreType.DMA((N_SEM,)),
        pltpu.SemaphoreType.DMA((4,)),
        pltpu.SemaphoreType.DMA,
        pltpu.SemaphoreType.DMA,
        pltpu.SemaphoreType.REGULAR,
    ]
    gain = norm_gain.reshape(1, D)
    turned, grad, rows = pl.pallas_call(
        kernel,
        out_shape=(
            pltpu.VMEM((NV, CB, ROWS), BF16),
            pltpu.VMEM((ROWS, COLS), BF16),
            pltpu.VMEM((NJ, 2, SB), F32),
        ),
        in_specs=[hbm] * 6,
        out_specs=(vmem, vmem, vmem),
        scratch_shapes=scratch,
        compiler_params=pltpu.CompilerParams(
            collective_id=0, has_side_effects=True, vmem_limit_bytes=LIMIT * 2**20
        ),
        name="distill_head",
    )(
        hidden,
        gain,
        teacher_slot.reshape(1, ROWS),
        valid_tokens.reshape(1, ROWS),
        head_weight.reshape(40, 128, COLS),
        teacher_logits.reshape(1024, COLS),
    )
    grad_hidden, grad_head = pl.pallas_call(
        finish_kernel,
        out_shape=(jax.ShapeDtypeStruct((2, D), BF16), jax.ShapeDtypeStruct((NV, CB, COLS), BF16)),
        in_specs=[hbm, hbm, vmem, vmem, vmem],
        out_specs=(hbm, hbm),
        scratch_shapes=[
            pltpu.VMEM((2, D), BF16),
            pltpu.VMEM((1, D), F32),
            pltpu.VMEM((2, D), BF16),
            pltpu.VMEM((NV, CB, COLS), BF16),
            pltpu.SemaphoreType.DMA((2,)),
            pltpu.SemaphoreType.DMA((NV + 1,)),
        ],
        compiler_params=pltpu.CompilerParams(vmem_limit_bytes=16 * 2**20),
        name="head_gradient",
    )(hidden, gain, rows, turned, grad)
    return grad_hidden, grad_head.reshape(D, COLS)


def solution(mesh):
    placed = (
        P(("seq", "vocab"), None),
        P(),
        P(None, ("seq", "vocab")),
        P("seq", None, "vocab"),
        P(),
        P(),
    )
    return jax.shard_map(
        shards,
        mesh=mesh,
        in_specs=placed,
        out_specs=(P(("seq", "vocab"), None), P(None, ("seq", "vocab"))),
        check_vma=False,
    )
```

```python
import functools

import jax
import jax.numpy as jnp
from jax import lax
from jax.experimental import pallas as pl
from jax.experimental.pallas import tpu as pltpu
from jax.sharding import PartitionSpec as P

MESH = pl.DeviceIdType.MESH
F32 = jnp.float32
BF16 = jnp.bfloat16
epsilon = 1e-06

NZ, NX, NY, NC = 8, 4, 4, 2
NV, NS = NY * NC, NZ * NX
ROWS, D, CB, SB, COLS = 512, 5120, 640, 1024, 512
HALF = ROWS // NC
NJ = 5
ORDER = (0, 2, 4, 1, 3)
XFIRST, YFIRST = (0, 1), (2, 3)
N_SEM = 240
LIMIT = 55
FIRST = 7
SPLIT = 6


class Links:
    def __init__(self, send, recv):
        self.send, self.recv, self.used = send, recv, 0

    def take(self, count=1):
        first = self.used
        self.used += count
        assert self.used <= N_SEM
        return first

    def copy(self, src, dst, device, index=None):
        if index is None:
            index = self.take()
        return pltpu.make_async_remote_copy(
            src_ref=src,
            dst_ref=dst,
            send_sem=self.send.at[index],
            recv_sem=self.recv.at[index],
            device_id=device,
            device_id_type=MESH,
        )


def mod(value, n):
    return lax.rem(value, n)


def loop(count, body):
    def step(i, carry):
        body(i)
        return carry

    lax.fori_loop(0, count, step, 0)


def kernel(
    hid_hbm, gain_hbm, slot_hbm, valid_hbm, w_hbm, teach_hbm,
    ft, grad, rows,
    hid, gain, slot, valid, w, teach, f, sf, zin, z32, t32, ts, tt, natural, column, onehot, logits, trow, st, sa, sb, sc,
    po, ps, cr, poz, psz, crz, tx, rx, ty, ry, tza, tzb, rz, ax, ay, az, t2, r2, tz2, rz2, a2, zz, a2z, yy,
    send, recv, isem, wsem, tsem, relayed,
):
    s = lax.axis_index("seq")
    v = lax.axis_index("vocab")
    z, x = lax.div(s, NX), mod(s, NX)
    y, c = lax.div(v, NC), mod(v, NC)
    links = Links(send, recv)

    def at_s(other):
        return (other, v)

    def at_v(other):
        return (s, other)

    def at_z(other):
        return (other * NX + x, v)

    def at_x(other):
        return (z * NX + other, v)

    def at_y(other):
        return (s, other * NC + c)

    wcopy = pltpu.make_async_copy(w_hbm, w, wsem)
    tcopy = pltpu.make_async_copy(teach_hbm, teach, tsem)
    inputs = [
        pltpu.make_async_copy(source, target, isem.at[i])
        for i, (source, target) in enumerate(((hid_hbm, hid), (gain_hbm, gain), (slot_hbm, slot), (valid_hbm, valid)))
    ]
    for copy in inputs:
        copy.start()
    tcopy.start()
    barrier = pltpu.get_barrier_semaphore()

    def greet_vocab(k):
        pl.semaphore_signal(barrier, inc=1, device_id=at_v(mod(v + k + 1, NV)), device_id_type=MESH)

    def greet_z(k):
        pl.semaphore_signal(barrier, inc=1, device_id=at_z(mod(z + k + 1, NZ)), device_id_type=MESH)

    def greet_x(k):
        pl.semaphore_signal(barrier, inc=1, device_id=at_x(mod(x + k + 1, NX)), device_id_type=MESH)

    loop(NX - 1, greet_x)
    loop(NZ - 1, greet_z)
    loop(NV - 1, greet_vocab)
    wcopy.start()

    for copy in inputs:
        copy.wait()
    h = hid[...].astype(F32)
    inv_rms = lax.rsqrt(jnp.mean(h * h, axis=1, keepdims=True) + epsilon)
    for b in range(NV):
        part = h[:, b * CB:(b + 1) * CB] * inv_rms * gain[:, b * CB:(b + 1) * CB]
        for i in range(2):
            sf[i * NV + b:i * NV + b + 1, :] = part[i:i + 1, :]
    zin[z] = sf[...].astype(BF16)
    pl.semaphore_wait(barrier, NX - 1 + NZ - 1 + NV - 1)

    z_first = links.take(NZ)
    teach_first = links.take(NS)

    def z_copy(k):
        return links.copy(zin.at[z], zin.at[z], at_z(mod(z + k, NZ)), z_first + k)

    def z_arrival(k):
        source = mod(z + NZ - k, NZ)
        return links.copy(zin.at[source], zin.at[source], at_z(source), z_first + k)

    def z_pair(i):
        z_copy(4 - i).start()
        z_copy(4 + i).start()

    z_copy(4).start()
    loop(3, lambda i: z_pair(i + 1))

    def relay(k):
        pl.semaphore_signal(relayed, inc=1, device_id=at_x(mod(x + k + 1, NX)), device_id_type=MESH)

    loop(NX - 1, relay)

    def teach_copy(dz, dx):
        to = mod(z + dz, NZ) * NX + mod(x + dx, NX)
        return links.copy(ts.at[to], tt.at[s], at_s(to), teach_first + dz * NX + dx)

    def teach_arrival(dz, dx):
        source = mod(z + NZ - dz, NZ) * NX + mod(x + NX - dx, NX)
        return links.copy(ts.at[source], tt.at[source], at_s(source), teach_first + dz * NX + dx)

    teach_order = [(dz, dx) for dx in (0, 1, 3, 2) for dz in (0, 1, 7, 2, 6, 3, 5, 4) if dz or dx]

    tcopy.wait()
    for b in range(4):
        t32[b] = teach[:, b * 128:(b + 1) * 128].astype(F32)

    def arrange(d):
        for b in range(4):
            ts[d, :, b * 128:(b + 1) * 128] = t32[b, pl.ds(d, 32, stride=NS), :].astype(BF16)

    loop(NS, arrange)
    tt[s] = ts[s]
    pl.semaphore_wait(relayed, NX - 1)
    for dz, dx in teach_order[:FIRST]:
        teach_copy(dz, dx).start()

    loop(NZ - 1, lambda k: z_arrival(k + 1).wait_recv())
    for b in range(CB // 128):
        z32[b] = zin[:, :, b * 128:(b + 1) * 128].astype(F32).reshape(NZ * 16, 128)
    for b in range(NV):
        for k in range(CB // 128):
            f[c, y, b, x, :, k * 128:(k + 1) * 128] = z32[k, pl.ds(b, 16, stride=NV), :].astype(BF16)

    offsets = (0, 1, 3, 2)
    other_core = (s, y * NC + (1 - c))
    pending, flushes = [], []

    def go(copy):
        copy.start()
        pending.append(copy)

    class Path:
        def __init__(self, span, x_last):
            self.span, self.x_last = span, x_last
            self.cut = (span[0] + span[1] + 1) // 2
            self.a, self.b = (y, x) if x_last else (x, y)
            self.to_a, self.to_b = (at_y, at_x) if x_last else (at_x, at_y)
            self.parts = [mod(self.a + 4 - o, 4) for o in offsets]
            self.up, self.down, self.far = mod(self.b + 1, 4), mod(self.b + 3, 4), mod(self.b + 2, 4)
            self.a_first, self.b_first, self.core_first = links.take(4), links.take(16), links.take(4)

        def ref(self, a, b, low=None, high=None):
            ya, xa = (a, b) if self.x_last else (b, a)
            low = self.span[0] if low is None else low
            high = self.span[1] if high is None else high
            return f.at[c, ya, low:high, xa]

        def a_copy(self, o, part):
            ref = self.ref(part, self.b)
            return links.copy(ref, ref, self.to_a(mod(self.a + o, 4)), self.a_first + o)

        def b_copy(self, kind, i, b, to, low=None, high=None):
            ref = self.ref(self.parts[i], b, low, high)
            return links.copy(ref, ref, self.to_b(to), self.b_first + kind * 4 + i)

        def own(self, i):
            go(self.b_copy(0, i, self.b, self.up))
            go(self.b_copy(1, i, self.b, self.down))

        def forward(self, i):
            self.b_copy(0, i, self.down, self.up).wait_recv()
            go(self.b_copy(2, i, self.down, self.up, None, self.cut))
            self.b_copy(1, i, self.up, self.down).wait_recv()
            go(self.b_copy(3, i, self.up, self.down, self.cut, None))

        def last(self, i):
            self.b_copy(2, i, self.far, self.up, None, self.cut).wait_recv()
            self.b_copy(3, i, self.far, self.down, self.cut, None).wait_recv()

        def core(self, rank, mine):
            b = (self.b, self.down, self.up, self.far)[rank]
            k = c if mine else 1 - c
            low, high = self.span
            ref = f.at[k, :, low:high, b] if self.x_last else f.at[k, b, low:high]
            return links.copy(ref, ref, other_core, self.core_first + rank)

    paths = (Path((0, SPLIT), False), Path((SPLIT, NV), True))
    for path in paths:
        for o in (1, 3, 2):
            go(path.a_copy(o, path.a))
    for path in paths:
        path.own(0)

    for dz, dx in teach_order[FIRST:]:
        teach_copy(dz, dx).start()

    quantity = lax.broadcasted_iota(jnp.int32, (128, ROWS), 0)
    natural[...] = jnp.where(quantity == 0, slot[...].astype(F32), valid[...].astype(F32)).T
    for k in range(NC * NY * NX * 2):
        kc, ky, kx, ki = k // 32, k // 8 % 4, k // 2 % 4, k % 2
        column[pl.ds(kc * 256 + ky * 64 + kx * 16 + ki, NZ, stride=2), :] = natural[
            pl.ds(kx * 16 + ky * 4 + kc * 2 + ki, NZ, stride=64), :]

    lane = lax.broadcasted_iota(jnp.int32, (ROWS, 128), 1).astype(F32)
    for b in range(8):
        onehot[:, b * 128:(b + 1) * 128] = jnp.where(column[:, 0:1] == lane + float(b * 128), 1.0, 0.0).astype(BF16)

    for i, o in enumerate(offsets):
        if o:
            for path in paths:
                path.a_copy(o, path.parts[i]).wait_recv()
                path.own(i)
    for path in paths:
        go(path.core(0, True))
    for i in range(4):
        for path in paths:
            path.forward(i)
    for path in paths:
        go(path.core(1, True))
        go(path.core(2, True))
    wcopy.wait()

    def multiply(half):
        logits[half] = jnp.zeros((HALF, COLS), F32)

        def block(b):
            fb = f[half, :, b].reshape(HALF, CB)
            wb = w[pl.ds(b * 5, 5)].reshape(CB, COLS)
            logits[half] += jnp.dot(fb, wb, preferred_element_type=F32)

        loop(NV, block)

    for path in paths:
        for i in range(4):
            path.last(i)
        go(path.core(3, True))
    multiply(c)
    for path in paths:
        for rank in range(4):
            path.core(rank, False).wait_recv()
    multiply(1 - c)

    for dz, dx in teach_order:
        teach_arrival(dz, dx).wait_recv()

    def select(i):
        span = pl.ds(pl.multiple_of(i * 256, 256), 256)
        trow[i] = jnp.dot(onehot[span, :], tt[...].reshape(1024, COLS), preferred_element_type=F32)

    loop(2, select)

    def statistics(i):
        span = pl.ds(pl.multiple_of(i * 64, 64), 64)
        inner = pl.ds(pl.multiple_of(mod(i, 4) * 64, 64), 64)
        lo, te = logits[lax.div(i, 4), inner, :], trow[lax.div(i, 4), inner, :]
        top = jnp.max(lo, axis=1, keepdims=True)
        teacher_top = jnp.max(te, axis=1, keepdims=True)
        e = jnp.exp(lo - top)
        total = jnp.sum(e, axis=1, keepdims=True)
        cross = jnp.sum(e * (lo - te), axis=1, keepdims=True)
        teacher_total = jnp.sum(jnp.exp(te - teacher_top), axis=1, keepdims=True)
        place = lax.broadcasted_iota(jnp.int32, (64, 128), 1)
        packed = jnp.where(place == 0, top + jnp.log(total), jnp.where(
            place == 1, teacher_top + jnp.log(teacher_total), jnp.where(place == 2, cross / total, 0.0)))
        st[span, :] = packed

    loop(8, statistics)

    def merged(ref):
        value = ref[...]

        def lse(part):
            top = jnp.max(part, axis=0)
            scale = jnp.exp(part - top[None])
            total = jnp.sum(scale, axis=0)
            return top + jnp.log(total), scale, total

        student_lse, scale, total = lse(value[:, 0:1, :])
        teacher_lse, _, _ = lse(value[:, 1:2, :])
        return student_lse, teacher_lse, jnp.sum(scale * value[:, 2:3, :], axis=0) / total

    def exchange(buffer, here, count, device, blocks):
        start = links.take(count)

        def out(k):
            return links.copy(buffer.at[here], buffer.at[here], device(mod(here + k, count)), start + k)

        def arrival(k):
            source = mod(here + count - k, count)
            return links.copy(buffer.at[source], buffer.at[source], device(source), start + k)

        loop(count - 1, lambda k: out(k + 1).start())
        for b in blocks:
            ft[b] = f[:, :, b].reshape(ROWS, CB).T
        loop(count - 1, lambda k: arrival(k + 1).wait_recv())
        return lambda: loop(count - 1, lambda k: out(k + 1).wait_send())

    def put(buffer, here, rows):
        for r, row in enumerate(rows):
            buffer[here, r:r + 1, :] = row

    sa[v] = st[...].T[0:4, :]
    flushes.append(exchange(sa, v, NV, at_v, (0, 1, 2)))
    put(sb, x, merged(sa))
    flushes.append(exchange(sb, x, NX, at_x, (3, 4)))
    put(sc, z, merged(sb))
    flushes.append(exchange(sc, z, NZ, at_z, (5, 6, 7)))
    student_lse, teacher_lse, mean_gap = merged(sc)
    divergence = mean_gap - student_lse + teacher_lse
    st[...] = jnp.where(quantity == 0, student_lse, jnp.where(quantity == 1, teacher_lse, jnp.where(
        quantity == 2, divergence, 0.0))).T

    def gradient(i):
        span = pl.ds(pl.multiple_of(i * 64, 64), 64)
        inner = pl.ds(pl.multiple_of(mod(i, 4) * 64, 64), 64)
        lo, te, q = logits[lax.div(i, 4), inner, :], trow[lax.div(i, 4), inner, :], st[span, :]
        shifted = lo - q[:, 0:1]
        gap = shifted - (te - q[:, 1:2])
        grad[span, :] = (column[span, 1:2] * jnp.exp(shifted) * (gap - q[:, 2:3])).astype(BF16)

    loop(8, gradient)

    def partial(j, half, ref):
        g = grad[pl.ds(pl.multiple_of(half * HALF, HALF), HALF), :]
        if j == 4:
            at = lax.broadcasted_iota(jnp.int32, (HALF, HALF), 0)
            source = (at // 2 % 4) * 64 + (at // 8 % 4) * 16 + (at // 32) * 2 + at % 2
            move = jnp.where(source == lax.broadcasted_iota(jnp.int32, (HALF, HALF), 1), 1.0, 0.0).astype(BF16)
            g = jnp.dot(move, g, preferred_element_type=F32).astype(BF16)
        for n in range(2):
            wn = w[j * 8 + n * 4:j * 8 + n * 4 + 4].reshape(512, COLS)
            product = lax.dot_general(g, wn, (((1,), (1,)), ((), ())), preferred_element_type=F32)
            if j == 4:
                ref[:, :, :, n * 512:(n + 1) * 512] = product.reshape(NZ, NX, 8, 512)
            else:
                ref[j, :, :, :, n * 512:(n + 1) * 512] = product.reshape(NY, NX, 16, 512)

    def add_core(j):
        def step(i):
            if j == 4:
                psz[i] += crz[i]
            else:
                ps[j, i] += cr[j, i]

        loop(NZ if j == 4 else NY, step)

    class Ring:
        def __init__(self, here, device, block, tmp, arrived):
            self.block, self.tmp, self.arrived, self.here = block, tmp, arrived, here
            up, down, far = mod(here + 1, 4), mod(here + 3, 4), mod(here + 2, 4)
            self.up, self.down = up, down
            self.far0 = links.copy(block(far, 0), tmp.at[0], device(up))
            self.far1 = links.copy(block(far, 1), tmp.at[1], device(down))
            self.free0 = links.copy(block(up, 1), arrived.at[0, 1], device(up))
            self.free1 = links.copy(block(down, 0), arrived.at[1, 0], device(down))
            self.last0 = links.copy(tmp.at[0], arrived.at[0, 0], device(up))
            self.last1 = links.copy(tmp.at[1], arrived.at[1, 1], device(down))
            for copy in (self.far0, self.far1, self.free0, self.free1):
                go(copy)

        def middle(self):
            self.far0.wait_recv()
            self.tmp[0] = self.tmp[0] + self.block(self.up, 0)[...]
            go(self.last0)
            self.far1.wait_recv()
            self.tmp[1] = self.tmp[1] + self.block(self.down, 1)[...]
            go(self.last1)

        def finish(self):
            for copy in (self.free0, self.free1, self.last0, self.last1):
                copy.wait_recv()
            return [self.block(self.here, i)[...] + self.arrived[0, i] + self.arrived[1, i] for i in (0, 1)]

    core_links = {j: links.copy(poz, crz, other_core) if j == 4 else links.copy(po.at[j], cr.at[j], other_core) for j in ORDER}
    stage1 = {}

    class Line:
        def __init__(self):
            p = [mod(z + k, NZ) for k in range(NZ)]
            self.p = p
            self.near = [links.copy(psz.at[p[1]], rz.at[0], at_z(p[1])), links.copy(psz.at[p[7]], rz.at[1], at_z(p[7]))]
            self.far = [
                links.copy(psz.at[p[3]], tza.at[0], at_z(p[1])),
                links.copy(psz.at[p[5]], tza.at[1], at_z(p[7])),
                links.copy(psz.at[p[4], 0:2], tzb.at[0], at_z(p[2])),
                links.copy(psz.at[p[4], 2:4], tzb.at[1], at_z(p[6])),
            ]
            self.summed = [links.copy(tza.at[0], rz.at[2], at_z(p[2])), links.copy(tza.at[1], rz.at[3], at_z(p[6]))]
            for copy in self.far + self.near:
                go(copy)

        def middle(self):
            for i, k in ((0, 2), (1, 6)):
                self.far[i].wait_recv()
                self.far[i + 2].wait_recv()
                tza[i] += psz[self.p[k]]
                tza[i, 2 * i:2 * i + 2] += tzb[i]
                go(self.summed[i])

        def finish(self):
            for copy in self.near + self.summed:
                copy.wait_recv()
            az[...] = psz[z] + rz[0] + rz[1] + rz[2] + rz[3]

    def begin(j):
        core_links[j].wait_recv()
        add_core(j)
        if j in XFIRST:
            stage1[j] = Ring(x, at_x, lambda i, half, j=j: ps.at[j, half * 2:half * 2 + 2, i], tx.at[j], rx.at[j])
        elif j in YFIRST:
            stage1[j] = Ring(y, at_y, lambda i, half, j=j: ps.at[j, i, half * 2:half * 2 + 2], ty.at[j - 2], ry.at[j - 2])
        else:
            stage1[j] = Line()

    for n, j in enumerate(ORDER):
        partial(j, 1 - c, poz if j == 4 else po)
        go(core_links[j])
        partial(j, c, psz if j == 4 else ps)
        if n:
            begin(ORDER[n - 1])
    begin(ORDER[-1])

    for j in (0, 2, 4, 1, 3):
        stage1[j].middle()

    def spread(buffer, source, here, count, device):
        start = links.take(count)

        def out(k):
            to = mod(here + k, count)
            return links.copy(source.at[to], buffer.at[here], device(to), start + k)

        def arrival(k):
            other = mod(here + count - k, count)
            return links.copy(source.at[other], buffer.at[other], device(other), start + k)

        loop(count - 1, lambda k: out(k + 1).start())
        buffer[here] = source[here]
        flushes.append(lambda: loop(count - 1, lambda k: out(k + 1).wait_send()))
        return lambda: loop(count - 1, lambda k: arrival(k + 1).wait_recv())

    stage2, stage3 = {}, {}

    def second(j):
        if j == 4:
            stage1[4].finish()
            stage2[4] = Ring(x, at_x, lambda i, half: az.at[i, :, half * 512:half * 512 + 512], tz2, rz2)
            return
        low, high = stage1[j].finish()
        mine = ax.at[j] if j in XFIRST else ay.at[j - 2]
        mine[0:2] = low
        mine[2:4] = high
        here, device = (y, at_y) if j in XFIRST else (x, at_x)
        stage2[j] = Ring(here, device, lambda i, half: mine.at[i, half * 8:half * 8 + 8], t2.at[j], r2.at[j])

    def third(j):
        low, high = stage2[j].finish()
        if j == 4:
            for k in range(NY):
                a2z[k, :, 0:512] = low[2 * k:2 * k + 2, :]
                a2z[k, :, 512:1024] = high[2 * k:2 * k + 2, :]
            stage3[j] = spread(yy, a2z, y, NY, at_y)
        else:
            for k in range(4):
                a2[j, k] = low[2 * k:2 * k + 2, :]
                a2[j, k + 4] = high[2 * k:2 * k + 2, :]
            stage3[j] = spread(zz.at[j], a2.at[j], z, NZ, at_z)

    for j in (0, 2, 1, 3, 4):
        second(j)
    for j in (0, 2, 1, 3, 4):
        stage2[j].middle()
    for j in (0, 2, 1, 3, 4):
        third(j)
    for j in (0, 2, 1, 3, 4):
        stage3[j]()
        rows[j] = jnp.sum(yy[...] if j == 4 else zz[j], axis=0)

    for copy in pending:
        copy.wait_send()
    loop(NZ - 1, lambda k: z_copy(k + 1).wait_send())
    for dz, dx in teach_order:
        teach_copy(dz, dx).wait_send()
    for flush in flushes:
        flush()


def finish_kernel(hid_hbm, gain_hbm, rows, ft, grad, gh_hbm, head_hbm, hid, gain, gh, stage, isem, osem):
    inputs = [pltpu.make_async_copy(hid_hbm, hid, isem.at[0]), pltpu.make_async_copy(gain_hbm, gain, isem.at[1])]
    outputs = [pltpu.make_async_copy(stage.at[b], head_hbm.at[b], osem.at[b]) for b in range(NV)]
    outputs.append(pltpu.make_async_copy(gh, gh_hbm, osem.at[NV]))
    for copy in inputs:
        copy.start()

    def head_block(b):
        stage[b] = jnp.dot(ft[b], grad[...], preferred_element_type=F32).astype(BF16)
        outputs[b].start()

    for b in range(4):
        head_block(b)
    for copy in inputs:
        copy.wait()
    h = hid[...].astype(F32)
    inv_rms = lax.rsqrt(jnp.mean(h * h, axis=1, keepdims=True) + epsilon)
    dots = jnp.zeros((2, 1), F32)
    for j in range(NJ):
        span = slice(j * SB, (j + 1) * SB)
        dots = dots + jnp.sum(rows[j] * gain[:, span] * (h[:, span] * inv_rms), axis=1, keepdims=True)
    dots = dots / D
    for j in range(NJ):
        span = slice(j * SB, (j + 1) * SB)
        gh[:, span] = (inv_rms * (rows[j] * gain[:, span] - h[:, span] * inv_rms * dots)).astype(BF16)
    outputs[NV].start()
    for b in range(4, NV):
        head_block(b)
    for copy in outputs:
        copy.wait()


def shards(hidden, norm_gain, head_weight, teacher_logits, teacher_slot, valid_tokens):
    vmem = pl.BlockSpec(memory_space=pltpu.VMEM)
    hbm = pl.BlockSpec(memory_space=pl.ANY)
    scratch = [
        pltpu.VMEM((2, D), BF16),
        pltpu.VMEM((1, D), F32),
        pltpu.VMEM((1, ROWS), jnp.int32),
        pltpu.VMEM((1, ROWS), jnp.int32),
        pltpu.VMEM((40, 128, COLS), BF16),
        pltpu.VMEM((1024, COLS), BF16),
        pltpu.VMEM((NC, NY, NV, NX, 16, CB), BF16),
        pltpu.VMEM((16, CB), F32),
        pltpu.VMEM((NZ, 16, CB), BF16),
        pltpu.VMEM((5, 128, 128), F32),
        pltpu.VMEM((4, 1024, 128), F32),
        pltpu.VMEM((NS, 32, COLS), BF16),
        pltpu.VMEM((NS, 32, COLS), BF16),
        pltpu.VMEM((ROWS, 128), F32),
        pltpu.VMEM((ROWS, 128), F32),
        pltpu.VMEM((ROWS, 1024), BF16),
        pltpu.VMEM((NC, HALF, COLS), F32),
        pltpu.VMEM((NC, HALF, COLS), F32),
        pltpu.VMEM((ROWS, 128), F32),
        pltpu.VMEM((NV, 4, ROWS), F32),
        pltpu.VMEM((NX, 4, ROWS), F32),
        pltpu.VMEM((NZ, 4, ROWS), F32),
        pltpu.VMEM((4, NY, NX, 16, SB), F32),
        pltpu.VMEM((4, NY, NX, 16, SB), F32),
        pltpu.VMEM((4, NY, NX, 16, SB), F32),
        pltpu.VMEM((NZ, NX, 8, SB), F32),
        pltpu.VMEM((NZ, NX, 8, SB), F32),
        pltpu.VMEM((NZ, NX, 8, SB), F32),
        pltpu.VMEM((2, 2, 2, 16, SB), F32),
        pltpu.VMEM((2, 2, 2, 2, 16, SB), F32),
        pltpu.VMEM((2, 2, 2, 16, SB), F32),
        pltpu.VMEM((2, 2, 2, 2, 16, SB), F32),
        pltpu.VMEM((2, NX, 8, SB), F32),
        pltpu.VMEM((2, 2, 8, SB), F32),
        pltpu.VMEM((4, NX, 8, SB), F32),
        pltpu.VMEM((2, NY, 16, SB), F32),
        pltpu.VMEM((2, NX, 16, SB), F32),
        pltpu.VMEM((NX, 8, SB), F32),
        pltpu.VMEM((4, 2, 8, SB), F32),
        pltpu.VMEM((4, 2, 2, 8, SB), F32),
        pltpu.VMEM((2, 8, SB // 2), F32),
        pltpu.VMEM((2, 2, 8, SB // 2), F32),
        pltpu.VMEM((4, NZ, 2, SB), F32),
        pltpu.VMEM((4, NZ, 2, SB), F32),
        pltpu.VMEM((NY, 2, SB), F32),
        pltpu.VMEM((NY, 2, SB), F32),
        pltpu.SemaphoreType.DMA((N_SEM,)),
        pltpu.SemaphoreType.DMA((N_SEM,)),
        pltpu.SemaphoreType.DMA((4,)),
        pltpu.SemaphoreType.DMA,
        pltpu.SemaphoreType.DMA,
        pltpu.SemaphoreType.REGULAR,
    ]
    gain = norm_gain.reshape(1, D)
    turned, grad, rows = pl.pallas_call(
        kernel,
        out_shape=(
            pltpu.VMEM((NV, CB, ROWS), BF16),
            pltpu.VMEM((ROWS, COLS), BF16),
            pltpu.VMEM((NJ, 2, SB), F32),
        ),
        in_specs=[hbm] * 6,
        out_specs=(vmem, vmem, vmem),
        scratch_shapes=scratch,
        compiler_params=pltpu.CompilerParams(
            collective_id=0, has_side_effects=True, vmem_limit_bytes=LIMIT * 2**20
        ),
        name="distill_head",
    )(
        hidden,
        gain,
        teacher_slot.reshape(1, ROWS),
        valid_tokens.reshape(1, ROWS),
        head_weight.reshape(40, 128, COLS),
        teacher_logits.reshape(1024, COLS),
    )
    grad_hidden, grad_head = pl.pallas_call(
        finish_kernel,
        out_shape=(jax.ShapeDtypeStruct((2, D), BF16), jax.ShapeDtypeStruct((NV, CB, COLS), BF16)),
        in_specs=[hbm, hbm, vmem, vmem, vmem],
        out_specs=(hbm, hbm),
        scratch_shapes=[
            pltpu.VMEM((2, D), BF16),
            pltpu.VMEM((1, D), F32),
            pltpu.VMEM((2, D), BF16),
            pltpu.VMEM((NV, CB, COLS), BF16),
            pltpu.SemaphoreType.DMA((2,)),
            pltpu.SemaphoreType.DMA((NV + 1,)),
        ],
        compiler_params=pltpu.CompilerParams(vmem_limit_bytes=16 * 2**20),
        name="head_gradient",
    )(hidden, gain, rows, turned, grad)
    return grad_hidden, grad_head.reshape(D, COLS)


def solution(mesh):
    placed = (
        P(("seq", "vocab"), None),
        P(),
        P(None, ("seq", "vocab")),
        P("seq", None, "vocab"),
        P(),
        P(),
    )
    return jax.shard_map(
        shards,
        mesh=mesh,
        in_specs=placed,
        out_specs=(P(("seq", "vocab"), None), P(None, ("seq", "vocab"))),
        check_vma=False,
    )
```

```python
import functools

import jax
import jax.numpy as jnp
from jax import lax
from jax.experimental import pallas as pl
from jax.experimental.pallas import tpu as pltpu
from jax.sharding import PartitionSpec as P

MESH = pl.DeviceIdType.MESH
F32 = jnp.float32
BF16 = jnp.bfloat16
epsilon = 1e-06

NZ, NX, NY, NC = 8, 4, 4, 2
NV, NS = NY * NC, NZ * NX
ROWS, D, CB, SB, COLS = 512, 5120, 640, 1024, 512
HALF = ROWS // NC
NJ = 5
ORDER = (0, 2, 4, 1, 3)
XFIRST, YFIRST = (0, 1), (2, 3)
N_SEM = 240
LIMIT = 55
FIRST = 15
SPLIT = 6


class Links:
    def __init__(self, send, recv):
        self.send, self.recv, self.used = send, recv, 0

    def take(self, count=1):
        first = self.used
        self.used += count
        assert self.used <= N_SEM
        return first

    def copy(self, src, dst, device, index=None):
        if index is None:
            index = self.take()
        return pltpu.make_async_remote_copy(
            src_ref=src,
            dst_ref=dst,
            send_sem=self.send.at[index],
            recv_sem=self.recv.at[index],
            device_id=device,
            device_id_type=MESH,
        )


def mod(value, n):
    return lax.rem(value, n)


def loop(count, body):
    def step(i, carry):
        body(i)
        return carry

    lax.fori_loop(0, count, step, 0)


def kernel(
    hid_hbm, gain_hbm, slot_hbm, valid_hbm, w_hbm, teach_hbm,
    ft, grad, rows,
    hid, gain, slot, valid, w, teach, f, sf, zin, z32, t32, ts, tt, natural, column, onehot, logits, trow, st, sa, sb, sc,
    po, ps, cr, poz, psz, crz, tx, rx, ty, ry, tza, tzb, rz, ax, ay, az, t2, r2, tz2, rz2, a2, zz, a2z, yy,
    send, recv, isem, wsem, tsem, relayed,
):
    s = lax.axis_index("seq")
    v = lax.axis_index("vocab")
    z, x = lax.div(s, NX), mod(s, NX)
    y, c = lax.div(v, NC), mod(v, NC)
    links = Links(send, recv)

    def at_s(other):
        return (other, v)

    def at_v(other):
        return (s, other)

    def at_z(other):
        return (other * NX + x, v)

    def at_x(other):
        return (z * NX + other, v)

    def at_y(other):
        return (s, other * NC + c)

    wcopy = pltpu.make_async_copy(w_hbm, w, wsem)
    tcopy = pltpu.make_async_copy(teach_hbm, teach, tsem)
    inputs = [
        pltpu.make_async_copy(source, target, isem.at[i])
        for i, (source, target) in enumerate(((hid_hbm, hid), (gain_hbm, gain), (slot_hbm, slot), (valid_hbm, valid)))
    ]
    for copy in inputs:
        copy.start()
    tcopy.start()
    barrier = pltpu.get_barrier_semaphore()

    def greet_vocab(k):
        pl.semaphore_signal(barrier, inc=1, device_id=at_v(mod(v + k + 1, NV)), device_id_type=MESH)

    def greet_z(k):
        pl.semaphore_signal(barrier, inc=1, device_id=at_z(mod(z + k + 1, NZ)), device_id_type=MESH)

    def greet_x(k):
        pl.semaphore_signal(barrier, inc=1, device_id=at_x(mod(x + k + 1, NX)), device_id_type=MESH)

    loop(NX - 1, greet_x)
    loop(NZ - 1, greet_z)
    loop(NV - 1, greet_vocab)
    wcopy.start()

    for copy in inputs:
        copy.wait()
    h = hid[...].astype(F32)
    inv_rms = lax.rsqrt(jnp.mean(h * h, axis=1, keepdims=True) + epsilon)
    for b in range(NV):
        part = h[:, b * CB:(b + 1) * CB] * inv_rms * gain[:, b * CB:(b + 1) * CB]
        for i in range(2):
            sf[i * NV + b:i * NV + b + 1, :] = part[i:i + 1, :]
    zin[z] = sf[...].astype(BF16)
    pl.semaphore_wait(barrier, NX - 1 + NZ - 1 + NV - 1)

    z_first = links.take(NZ)
    teach_first = links.take(NS)

    def z_copy(k):
        return links.copy(zin.at[z], zin.at[z], at_z(mod(z + k, NZ)), z_first + k)

    def z_arrival(k):
        source = mod(z + NZ - k, NZ)
        return links.copy(zin.at[source], zin.at[source], at_z(source), z_first + k)

    def z_pair(i):
        z_copy(4 - i).start()
        z_copy(4 + i).start()

    z_copy(4).start()
    loop(3, lambda i: z_pair(i + 1))

    def relay(k):
        pl.semaphore_signal(relayed, inc=1, device_id=at_x(mod(x + k + 1, NX)), device_id_type=MESH)

    loop(NX - 1, relay)

    def teach_copy(dz, dx):
        to = mod(z + dz, NZ) * NX + mod(x + dx, NX)
        return links.copy(ts.at[to], tt.at[s], at_s(to), teach_first + dz * NX + dx)

    def teach_arrival(dz, dx):
        source = mod(z + NZ - dz, NZ) * NX + mod(x + NX - dx, NX)
        return links.copy(ts.at[source], tt.at[source], at_s(source), teach_first + dz * NX + dx)

    teach_order = [(dz, dx) for dx in (0, 1, 3, 2) for dz in (0, 1, 7, 2, 6, 3, 5, 4) if dz or dx]

    tcopy.wait()
    for b in range(4):
        t32[b] = teach[:, b * 128:(b + 1) * 128].astype(F32)

    def arrange(d):
        for b in range(4):
            ts[d, :, b * 128:(b + 1) * 128] = t32[b, pl.ds(d, 32, stride=NS), :].astype(BF16)

    loop(NS, arrange)
    tt[s] = ts[s]
    pl.semaphore_wait(relayed, NX - 1)
    for dz, dx in teach_order[:FIRST]:
        teach_copy(dz, dx).start()

    loop(NZ - 1, lambda k: z_arrival(k + 1).wait_recv())
    for b in range(CB // 128):
        z32[b] = zin[:, :, b * 128:(b + 1) * 128].astype(F32).reshape(NZ * 16, 128)
    for b in range(NV):
        for k in range(CB // 128):
            f[c, y, b, x, :, k * 128:(k + 1) * 128] = z32[k, pl.ds(b, 16, stride=NV), :].astype(BF16)

    offsets = (0, 1, 3, 2)
    other_core = (s, y * NC + (1 - c))
    pending, flushes = [], []

    def go(copy):
        copy.start()
        pending.append(copy)

    class Path:
        def __init__(self, span, x_last):
            self.span, self.x_last = span, x_last
            self.cut = (span[0] + span[1] + 1) // 2
            self.a, self.b = (y, x) if x_last else (x, y)
            self.to_a, self.to_b = (at_y, at_x) if x_last else (at_x, at_y)
            self.parts = [mod(self.a + 4 - o, 4) for o in offsets]
            self.up, self.down, self.far = mod(self.b + 1, 4), mod(self.b + 3, 4), mod(self.b + 2, 4)
            self.a_first, self.b_first, self.core_first = links.take(4), links.take(16), links.take(4)

        def ref(self, a, b, low=None, high=None):
            ya, xa = (a, b) if self.x_last else (b, a)
            low = self.span[0] if low is None else low
            high = self.span[1] if high is None else high
            return f.at[c, ya, low:high, xa]

        def a_copy(self, o, part):
            ref = self.ref(part, self.b)
            return links.copy(ref, ref, self.to_a(mod(self.a + o, 4)), self.a_first + o)

        def b_copy(self, kind, i, b, to, low=None, high=None):
            ref = self.ref(self.parts[i], b, low, high)
            return links.copy(ref, ref, self.to_b(to), self.b_first + kind * 4 + i)

        def own(self, i):
            go(self.b_copy(0, i, self.b, self.up))
            go(self.b_copy(1, i, self.b, self.down))

        def forward(self, i):
            self.b_copy(0, i, self.down, self.up).wait_recv()
            go(self.b_copy(2, i, self.down, self.up, None, self.cut))
            self.b_copy(1, i, self.up, self.down).wait_recv()
            go(self.b_copy(3, i, self.up, self.down, self.cut, None))

        def last(self, i):
            self.b_copy(2, i, self.far, self.up, None, self.cut).wait_recv()
            self.b_copy(3, i, self.far, self.down, self.cut, None).wait_recv()

        def core(self, rank, mine):
            b = (self.b, self.down, self.up, self.far)[rank]
            k = c if mine else 1 - c
            low, high = self.span
            ref = f.at[k, :, low:high, b] if self.x_last else f.at[k, b, low:high]
            return links.copy(ref, ref, other_core, self.core_first + rank)

    paths = (Path((0, SPLIT), False), Path((SPLIT, NV), True))
    for path in paths:
        for o in (1, 3, 2):
            go(path.a_copy(o, path.a))
    for path in paths:
        path.own(0)

    for dz, dx in teach_order[FIRST:]:
        teach_copy(dz, dx).start()

    quantity = lax.broadcasted_iota(jnp.int32, (128, ROWS), 0)
    natural[...] = jnp.where(quantity == 0, slot[...].astype(F32), valid[...].astype(F32)).T
    for k in range(NC * NY * NX * 2):
        kc, ky, kx, ki = k // 32, k // 8 % 4, k // 2 % 4, k % 2
        column[pl.ds(kc * 256 + ky * 64 + kx * 16 + ki, NZ, stride=2), :] = natural[
            pl.ds(kx * 16 + ky * 4 + kc * 2 + ki, NZ, stride=64), :]

    lane = lax.broadcasted_iota(jnp.int32, (ROWS, 128), 1).astype(F32)
    for b in range(8):
        onehot[:, b * 128:(b + 1) * 128] = jnp.where(column[:, 0:1] == lane + float(b * 128), 1.0, 0.0).astype(BF16)

    for i, o in enumerate(offsets):
        if o:
            for path in paths:
                path.a_copy(o, path.parts[i]).wait_recv()
                path.own(i)
    for path in paths:
        go(path.core(0, True))
    for i in range(4):
        for path in paths:
            path.forward(i)
    for path in paths:
        go(path.core(1, True))
        go(path.core(2, True))
    wcopy.wait()

    def multiply(half):
        logits[half] = jnp.zeros((HALF, COLS), F32)

        def block(b):
            fb = f[half, :, b].reshape(HALF, CB)
            wb = w[pl.ds(b * 5, 5)].reshape(CB, COLS)
            logits[half] += jnp.dot(fb, wb, preferred_element_type=F32)

        loop(NV, block)

    for path in paths:
        for i in range(4):
            path.last(i)
        go(path.core(3, True))
    multiply(c)
    for path in paths:
        for rank in range(4):
            path.core(rank, False).wait_recv()
    multiply(1 - c)

    for dz, dx in teach_order:
        teach_arrival(dz, dx).wait_recv()

    def select(i):
        span = pl.ds(pl.multiple_of(i * 256, 256), 256)
        trow[i] = jnp.dot(onehot[span, :], tt[...].reshape(1024, COLS), preferred_element_type=F32)

    loop(2, select)

    def statistics(i):
        span = pl.ds(pl.multiple_of(i * 64, 64), 64)
        inner = pl.ds(pl.multiple_of(mod(i, 4) * 64, 64), 64)
        lo, te = logits[lax.div(i, 4), inner, :], trow[lax.div(i, 4), inner, :]
        top = jnp.max(lo, axis=1, keepdims=True)
        teacher_top = jnp.max(te, axis=1, keepdims=True)
        e = jnp.exp(lo - top)
        total = jnp.sum(e, axis=1, keepdims=True)
        cross = jnp.sum(e * (lo - te), axis=1, keepdims=True)
        teacher_total = jnp.sum(jnp.exp(te - teacher_top), axis=1, keepdims=True)
        place = lax.broadcasted_iota(jnp.int32, (64, 128), 1)
        packed = jnp.where(place == 0, top + jnp.log(total), jnp.where(
            place == 1, teacher_top + jnp.log(teacher_total), jnp.where(place == 2, cross / total, 0.0)))
        st[span, :] = packed

    loop(8, statistics)

    def merged(ref):
        value = ref[...]

        def lse(part):
            top = jnp.max(part, axis=0)
            scale = jnp.exp(part - top[None])
            total = jnp.sum(scale, axis=0)
            return top + jnp.log(total), scale, total

        student_lse, scale, total = lse(value[:, 0:1, :])
        teacher_lse, _, _ = lse(value[:, 1:2, :])
        return student_lse, teacher_lse, jnp.sum(scale * value[:, 2:3, :], axis=0) / total

    def exchange(buffer, here, count, device, blocks):
        start = links.take(count)

        def out(k):
            return links.copy(buffer.at[here], buffer.at[here], device(mod(here + k, count)), start + k)

        def arrival(k):
            source = mod(here + count - k, count)
            return links.copy(buffer.at[source], buffer.at[source], device(source), start + k)

        for k in sorted(range(1, count), key=lambda k: -min(k, count - k)):
            out(k).start()
        for b in blocks:
            ft[b] = f[:, :, b].reshape(ROWS, CB).T
        loop(count - 1, lambda k: arrival(k + 1).wait_recv())
        return lambda: loop(count - 1, lambda k: out(k + 1).wait_send())

    def put(buffer, here, rows):
        for r, row in enumerate(rows):
            buffer[here, r:r + 1, :] = row

    sa[v] = st[...].T[0:4, :]
    flushes.append(exchange(sa, v, NV, at_v, (0, 1, 2)))
    put(sb, x, merged(sa))
    flushes.append(exchange(sb, x, NX, at_x, (3, 4)))
    put(sc, z, merged(sb))
    flushes.append(exchange(sc, z, NZ, at_z, (5, 6, 7)))
    student_lse, teacher_lse, mean_gap = merged(sc)
    divergence = mean_gap - student_lse + teacher_lse
    st[...] = jnp.where(quantity == 0, student_lse, jnp.where(quantity == 1, teacher_lse, jnp.where(
        quantity == 2, divergence, 0.0))).T

    def gradient(i):
        span = pl.ds(pl.multiple_of(i * 64, 64), 64)
        inner = pl.ds(pl.multiple_of(mod(i, 4) * 64, 64), 64)
        lo, te, q = logits[lax.div(i, 4), inner, :], trow[lax.div(i, 4), inner, :], st[span, :]
        shifted = lo - q[:, 0:1]
        gap = shifted - (te - q[:, 1:2])
        grad[span, :] = (column[span, 1:2] * jnp.exp(shifted) * (gap - q[:, 2:3])).astype(BF16)

    loop(8, gradient)

    def partial(j, half, ref):
        g = grad[pl.ds(pl.multiple_of(half * HALF, HALF), HALF), :]
        if j == 4:
            at = lax.broadcasted_iota(jnp.int32, (HALF, HALF), 0)
            source = (at // 2 % 4) * 64 + (at // 8 % 4) * 16 + (at // 32) * 2 + at % 2
            move = jnp.where(source == lax.broadcasted_iota(jnp.int32, (HALF, HALF), 1), 1.0, 0.0).astype(BF16)
            g = jnp.dot(move, g, preferred_element_type=F32).astype(BF16)
        for n in range(2):
            wn = w[j * 8 + n * 4:j * 8 + n * 4 + 4].reshape(512, COLS)
            product = lax.dot_general(g, wn, (((1,), (1,)), ((), ())), preferred_element_type=F32)
            if j == 4:
                ref[:, :, :, n * 512:(n + 1) * 512] = product.reshape(NZ, NX, 8, 512)
            else:
                ref[j, :, :, :, n * 512:(n + 1) * 512] = product.reshape(NY, NX, 16, 512)

    def add_core(j):
        def step(i):
            if j == 4:
                psz[i] += crz[i]
            else:
                ps[j, i] += cr[j, i]

        loop(NZ if j == 4 else NY, step)

    class Ring:
        def __init__(self, here, device, block, tmp, arrived):
            self.block, self.tmp, self.arrived, self.here = block, tmp, arrived, here
            up, down, far = mod(here + 1, 4), mod(here + 3, 4), mod(here + 2, 4)
            self.up, self.down = up, down
            self.far0 = links.copy(block(far, 0), tmp.at[0], device(up))
            self.far1 = links.copy(block(far, 1), tmp.at[1], device(down))
            self.free0 = links.copy(block(up, 1), arrived.at[0, 1], device(up))
            self.free1 = links.copy(block(down, 0), arrived.at[1, 0], device(down))
            self.last0 = links.copy(tmp.at[0], arrived.at[0, 0], device(up))
            self.last1 = links.copy(tmp.at[1], arrived.at[1, 1], device(down))
            for copy in (self.far0, self.far1, self.free0, self.free1):
                go(copy)

        def middle(self):
            self.far0.wait_recv()
            self.tmp[0] = self.tmp[0] + self.block(self.up, 0)[...]
            go(self.last0)
            self.far1.wait_recv()
            self.tmp[1] = self.tmp[1] + self.block(self.down, 1)[...]
            go(self.last1)

        def finish(self):
            for copy in (self.free0, self.free1, self.last0, self.last1):
                copy.wait_recv()
            return [self.block(self.here, i)[...] + self.arrived[0, i] + self.arrived[1, i] for i in (0, 1)]

    core_links = {j: links.copy(poz, crz, other_core) if j == 4 else links.copy(po.at[j], cr.at[j], other_core) for j in ORDER}
    stage1 = {}

    class Line:
        def __init__(self):
            p = [mod(z + k, NZ) for k in range(NZ)]
            self.p = p
            self.near = [links.copy(psz.at[p[1]], rz.at[0], at_z(p[1])), links.copy(psz.at[p[7]], rz.at[1], at_z(p[7]))]
            self.far = [
                links.copy(psz.at[p[3]], tza.at[0], at_z(p[1])),
                links.copy(psz.at[p[5]], tza.at[1], at_z(p[7])),
                links.copy(psz.at[p[4], 0:2], tzb.at[0], at_z(p[2])),
                links.copy(psz.at[p[4], 2:4], tzb.at[1], at_z(p[6])),
            ]
            self.summed = [links.copy(tza.at[0], rz.at[2], at_z(p[2])), links.copy(tza.at[1], rz.at[3], at_z(p[6]))]
            for copy in self.far + self.near:
                go(copy)

        def middle(self):
            for i, k in ((0, 2), (1, 6)):
                self.far[i].wait_recv()
                self.far[i + 2].wait_recv()
                tza[i] += psz[self.p[k]]
                tza[i, 2 * i:2 * i + 2] += tzb[i]
                go(self.summed[i])

        def finish(self):
            for copy in self.near + self.summed:
                copy.wait_recv()
            az[...] = psz[z] + rz[0] + rz[1] + rz[2] + rz[3]

    def begin(j):
        core_links[j].wait_recv()
        add_core(j)
        if j in XFIRST:
            stage1[j] = Ring(x, at_x, lambda i, half, j=j: ps.at[j, half * 2:half * 2 + 2, i], tx.at[j], rx.at[j])
        elif j in YFIRST:
            stage1[j] = Ring(y, at_y, lambda i, half, j=j: ps.at[j, i, half * 2:half * 2 + 2], ty.at[j - 2], ry.at[j - 2])
        else:
            stage1[j] = Line()

    def other_half(j):
        partial(j, 1 - c, poz if j == 4 else po)
        go(core_links[j])

    other_half(ORDER[0])
    for n, j in enumerate(ORDER):
        if n + 1 < len(ORDER):
            other_half(ORDER[n + 1])
        partial(j, c, psz if j == 4 else ps)
        if n + 1 < len(ORDER):
            begin(j)
    begin(ORDER[-1])

    for j in (0, 2, 4, 1, 3):
        stage1[j].middle()

    def spread(buffer, source, here, count, device):
        start = links.take(count)

        def out(k):
            to = mod(here + k, count)
            return links.copy(source.at[to], buffer.at[here], device(to), start + k)

        def arrival(k):
            other = mod(here + count - k, count)
            return links.copy(source.at[other], buffer.at[other], device(other), start + k)

        for k in sorted(range(1, count), key=lambda k: -min(k, count - k)):
            out(k).start()
        buffer[here] = source[here]
        flushes.append(lambda: loop(count - 1, lambda k: out(k + 1).wait_send()))
        return lambda: loop(count - 1, lambda k: arrival(k + 1).wait_recv())

    stage2, stage3 = {}, {}

    def second(j):
        if j == 4:
            stage1[4].finish()
            stage2[4] = Ring(x, at_x, lambda i, half: az.at[i, :, half * 512:half * 512 + 512], tz2, rz2)
            return
        low, high = stage1[j].finish()
        mine = ax.at[j] if j in XFIRST else ay.at[j - 2]
        mine[0:2] = low
        mine[2:4] = high
        here, device = (y, at_y) if j in XFIRST else (x, at_x)
        stage2[j] = Ring(here, device, lambda i, half: mine.at[i, half * 8:half * 8 + 8], t2.at[j], r2.at[j])

    def third(j):
        low, high = stage2[j].finish()
        if j == 4:
            for k in range(NY):
                a2z[k, :, 0:512] = low[2 * k:2 * k + 2, :]
                a2z[k, :, 512:1024] = high[2 * k:2 * k + 2, :]
            stage3[j] = spread(yy, a2z, y, NY, at_y)
        else:
            for k in range(4):
                a2[j, k] = low[2 * k:2 * k + 2, :]
                a2[j, k + 4] = high[2 * k:2 * k + 2, :]
            stage3[j] = spread(zz.at[j], a2.at[j], z, NZ, at_z)

    for j in (0, 2, 1, 3, 4):
        second(j)
    for j in (0, 2, 1, 3, 4):
        stage2[j].middle()
    for j in (0, 2, 1, 3, 4):
        third(j)
    for j in (0, 2, 1, 3, 4):
        stage3[j]()
        rows[j] = jnp.sum(yy[...] if j == 4 else zz[j], axis=0)

    for copy in pending:
        copy.wait_send()
    loop(NZ - 1, lambda k: z_copy(k + 1).wait_send())
    for dz, dx in teach_order:
        teach_copy(dz, dx).wait_send()
    for flush in flushes:
        flush()


def finish_kernel(hid_hbm, gain_hbm, rows, ft, grad, gh_hbm, head_hbm, hid, gain, gh, stage, isem, osem):
    inputs = [pltpu.make_async_copy(hid_hbm, hid, isem.at[0]), pltpu.make_async_copy(gain_hbm, gain, isem.at[1])]
    outputs = [pltpu.make_async_copy(stage.at[b], head_hbm.at[b], osem.at[b]) for b in range(NV)]
    outputs.append(pltpu.make_async_copy(gh, gh_hbm, osem.at[NV]))
    for copy in inputs:
        copy.start()

    def head_block(b):
        stage[b] = jnp.dot(ft[b], grad[...], preferred_element_type=F32).astype(BF16)
        outputs[b].start()

    for b in range(4):
        head_block(b)
    for copy in inputs:
        copy.wait()
    h = hid[...].astype(F32)
    inv_rms = lax.rsqrt(jnp.mean(h * h, axis=1, keepdims=True) + epsilon)
    dots = jnp.zeros((2, 1), F32)
    for j in range(NJ):
        span = slice(j * SB, (j + 1) * SB)
        dots = dots + jnp.sum(rows[j] * gain[:, span] * (h[:, span] * inv_rms), axis=1, keepdims=True)
    dots = dots / D
    for j in range(NJ):
        span = slice(j * SB, (j + 1) * SB)
        gh[:, span] = (inv_rms * (rows[j] * gain[:, span] - h[:, span] * inv_rms * dots)).astype(BF16)
    outputs[NV].start()
    for b in range(4, NV):
        head_block(b)
    for copy in outputs:
        copy.wait()


def shards(hidden, norm_gain, head_weight, teacher_logits, teacher_slot, valid_tokens):
    vmem = pl.BlockSpec(memory_space=pltpu.VMEM)
    hbm = pl.BlockSpec(memory_space=pl.ANY)
    scratch = [
        pltpu.VMEM((2, D), BF16),
        pltpu.VMEM((1, D), F32),
        pltpu.VMEM((1, ROWS), jnp.int32),
        pltpu.VMEM((1, ROWS), jnp.int32),
        pltpu.VMEM((40, 128, COLS), BF16),
        pltpu.VMEM((1024, COLS), BF16),
        pltpu.VMEM((NC, NY, NV, NX, 16, CB), BF16),
        pltpu.VMEM((16, CB), F32),
        pltpu.VMEM((NZ, 16, CB), BF16),
        pltpu.VMEM((5, 128, 128), F32),
        pltpu.VMEM((4, 1024, 128), F32),
        pltpu.VMEM((NS, 32, COLS), BF16),
        pltpu.VMEM((NS, 32, COLS), BF16),
        pltpu.VMEM((ROWS, 128), F32),
        pltpu.VMEM((ROWS, 128), F32),
        pltpu.VMEM((ROWS, 1024), BF16),
        pltpu.VMEM((NC, HALF, COLS), F32),
        pltpu.VMEM((NC, HALF, COLS), F32),
        pltpu.VMEM((ROWS, 128), F32),
        pltpu.VMEM((NV, 4, ROWS), F32),
        pltpu.VMEM((NX, 4, ROWS), F32),
        pltpu.VMEM((NZ, 4, ROWS), F32),
        pltpu.VMEM((4, NY, NX, 16, SB), F32),
        pltpu.VMEM((4, NY, NX, 16, SB), F32),
        pltpu.VMEM((4, NY, NX, 16, SB), F32),
        pltpu.VMEM((NZ, NX, 8, SB), F32),
        pltpu.VMEM((NZ, NX, 8, SB), F32),
        pltpu.VMEM((NZ, NX, 8, SB), F32),
        pltpu.VMEM((2, 2, 2, 16, SB), F32),
        pltpu.VMEM((2, 2, 2, 2, 16, SB), F32),
        pltpu.VMEM((2, 2, 2, 16, SB), F32),
        pltpu.VMEM((2, 2, 2, 2, 16, SB), F32),
        pltpu.VMEM((2, NX, 8, SB), F32),
        pltpu.VMEM((2, 2, 8, SB), F32),
        pltpu.VMEM((4, NX, 8, SB), F32),
        pltpu.VMEM((2, NY, 16, SB), F32),
        pltpu.VMEM((2, NX, 16, SB), F32),
        pltpu.VMEM((NX, 8, SB), F32),
        pltpu.VMEM((4, 2, 8, SB), F32),
        pltpu.VMEM((4, 2, 2, 8, SB), F32),
        pltpu.VMEM((2, 8, SB // 2), F32),
        pltpu.VMEM((2, 2, 8, SB // 2), F32),
        pltpu.VMEM((4, NZ, 2, SB), F32),
        pltpu.VMEM((4, NZ, 2, SB), F32),
        pltpu.VMEM((NY, 2, SB), F32),
        pltpu.VMEM((NY, 2, SB), F32),
        pltpu.SemaphoreType.DMA((N_SEM,)),
        pltpu.SemaphoreType.DMA((N_SEM,)),
        pltpu.SemaphoreType.DMA((4,)),
        pltpu.SemaphoreType.DMA,
        pltpu.SemaphoreType.DMA,
        pltpu.SemaphoreType.REGULAR,
    ]
    gain = norm_gain.reshape(1, D)
    turned, grad, rows = pl.pallas_call(
        kernel,
        out_shape=(
            pltpu.VMEM((NV, CB, ROWS), BF16),
            pltpu.VMEM((ROWS, COLS), BF16),
            pltpu.VMEM((NJ, 2, SB), F32),
        ),
        in_specs=[hbm] * 6,
        out_specs=(vmem, vmem, vmem),
        scratch_shapes=scratch,
        compiler_params=pltpu.CompilerParams(
            collective_id=0, has_side_effects=True, vmem_limit_bytes=LIMIT * 2**20
        ),
        name="distill_head",
    )(
        hidden,
        gain,
        teacher_slot.reshape(1, ROWS),
        valid_tokens.reshape(1, ROWS),
        head_weight.reshape(40, 128, COLS),
        teacher_logits.reshape(1024, COLS),
    )
    grad_hidden, grad_head = pl.pallas_call(
        finish_kernel,
        out_shape=(jax.ShapeDtypeStruct((2, D), BF16), jax.ShapeDtypeStruct((NV, CB, COLS), BF16)),
        in_specs=[hbm, hbm, vmem, vmem, vmem],
        out_specs=(hbm, hbm),
        scratch_shapes=[
            pltpu.VMEM((2, D), BF16),
            pltpu.VMEM((1, D), F32),
            pltpu.VMEM((2, D), BF16),
            pltpu.VMEM((NV, CB, COLS), BF16),
            pltpu.SemaphoreType.DMA((2,)),
            pltpu.SemaphoreType.DMA((NV + 1,)),
        ],
        compiler_params=pltpu.CompilerParams(vmem_limit_bytes=16 * 2**20),
        name="head_gradient",
    )(hidden, gain, rows, turned, grad)
    return grad_hidden, grad_head.reshape(D, COLS)


def solution(mesh):
    placed = (
        P(("seq", "vocab"), None),
        P(),
        P(None, ("seq", "vocab")),
        P("seq", None, "vocab"),
        P(),
        P(),
    )
    return jax.shard_map(
        shards,
        mesh=mesh,
        in_specs=placed,
        out_specs=(P(("seq", "vocab"), None), P(None, ("seq", "vocab"))),
        check_vma=False,
    )
```
